256 devices in a mesh: dp: 4 (over x_hi, core), section: 8 (over x_lo, y), tensor: 8 (over z).
Axes of the slice: x: 4 (x_hi: 2, x_lo: 2; x = x_hi * 2 + x_lo), y: 4, z: 8, core: 2. Of those that a mesh axis runs over, the one named last changes fastest.
Arguments:
- text: bfloat16 [8, 64, 8192], P('dp', None, 'tensor'), may hold values from -6 to 6
- order: int32 [4, 2], P('dp'), may hold values from 0 to 1, each once within a row
- lengths: int32 [4, 2], P('dp'), may hold values from 16 to 64
- image: bfloat16 [8, 32, 8192], P('dp', 'section', 'tensor'), may hold values from -6 to 6
- in_gain: float32 [8, 8192], P('section'), may hold values from 0.25 to 1.75
- wq: bfloat16 [8, 8192, 4096], P('section', 'dp', 'tensor'), may hold values from -0.0625 to 0.0625
- wk: bfloat16 [8, 8192, 1024], P('section', 'dp', 'tensor'), may hold values from -0.0625 to 0.0625
- wv: bfloat16 [8, 8192, 1024], P('section', 'dp', 'tensor'), may hold values from -0.0625 to 0.0625
- wo: bfloat16 [8, 4096, 8192], P('section', 'tensor', 'dp'), may hold values from -0.09375 to 0.09375
- query_norm_gain: float32 [8, 128], P('section'), may hold values from 0.5 to 2
- k_gain: float32 [8, 128], P('section'), may hold values from 0.5 to 2
- gate: float32 [8], P('section'), may hold values from -1.5 to 1.5
- cot: bfloat16 [8, 8, 64, 8192], P('section', 'dp'), may hold values from -6 to 6
Outputs:
- states: bfloat16 [8, 8, 64, 8192], P('section', 'dp', None, 'tensor')
- image_grad: float32 [8, 32, 8192], P('dp', 'section', 'tensor')
The draws below stay inside these ranges and needn't reach their ends.
Inputs may be any that keep to these rules, and one draw needn't show every extreme that they name: `order`: each row lists the 2 micro-batches of one data-parallel group, each once.
All inputs are finite; a program needn't handle non-finite values.
Results may differ from the reference program's by a relative error of at most 0.035.
Values may be sent and summed in bfloat16 or wider, within the bound.
No kernel may reach another device: no remote copies, remote signals or barrier semaphores. Data moves between devices by JAX's collectives and lax.ppermute only.
A program may use at most 128 MiB of HBM per device.

```python
import math
import jax
import jax.numpy as jnp
from jax import lax

MODEL_WIDTH = 8192
QUERY_HEADS = 32
KEY_VALUE_HEADS = 8
HEAD_SIZE = 128
TEXT_ROWS = 64
MB_DEV = 2
IMAGE_TOKEN_ROWS = 32
MB = 8
N_DP = 4
N_SECTION = 8
N_TENSOR = 8


def spread_gain(key, lower, upper):
    unit = jax.random.uniform(key, (N_SECTION, HEAD_SIZE), jnp.float32)
    return jnp.exp(math.log(lower) + unit * (math.log(upper) - math.log(lower)))


def draw_query_norm_gain(key, part):
    key = jax.random.fold_in(key, 11)
    return spread_gain(key, 0.5, 1.5)


def draw_k_gain(key, part):
    key = jax.random.fold_in(key, 12)
    return spread_gain(key, 0.5, 1.5)


def touch_ends(entries, key, smallest, high):
    longest = entries.shape.index(max(entries.shape))
    spots = []
    for shift in (0, 1):
        where = [jax.random.randint(jax.random.fold_in(key, axis), (), 0, length) for axis, length in enumerate(entries.shape)]
        where[longest] = (where[longest] + shift) % entries.shape[longest]
        spots.append(tuple(where))
    return entries.at[spots[0]].set(smallest).at[spots[1]].set(high)


def shard_levels(own_key, shape, pieces, least, high):
    loudness, own = 1.0, jax.random.fold_in(own_key, 6)
    for position, blocks in pieces:
        heights = jnp.exp(jax.random.uniform(jax.random.fold_in(own, position), (blocks,), jnp.float32, least / len(pieces), high / len(pieces)))
        loudness = loudness * jnp.repeat(heights, shape[position] // blocks).reshape([-1 if axis == position else 1 for axis in range(len(shape))])
    return loudness


def gaussian(stream_key, shape, spread, limit, pieces=(), held_as=jnp.bfloat16):
    drawn = jax.random.normal(stream_key, shape, jnp.float32) * spread
    if len(pieces) > 0:
        drawn = shard_levels(stream_key, shape, pieces, -0.22, 0.18) * drawn
    return jnp.clip(drawn, min=-limit, max=limit).astype(held_as)


def setup_inputs(seed: int = 0) -> dict:
    streams_of = jax.random.split(jax.random.key(seed), 14)
    text = gaussian(streams_of[0], (MB, TEXT_ROWS, MODEL_WIDTH), 1.0, 6.0, ((0, 4), (2, 8)))
    order = jax.vmap(lambda own: jax.random.permutation(own, MB_DEV))(jax.random.split(streams_of[1], N_DP)).reshape((N_DP, MB_DEV)).astype(jnp.int32)
    lengths = touch_ends(jax.random.randint(streams_of[2], (N_DP, MB_DEV), TEXT_ROWS // 4, TEXT_ROWS + 1), jax.random.fold_in(streams_of[2], 1), TEXT_ROWS // 4, TEXT_ROWS).astype(jnp.int32)
    image = gaussian(streams_of[3], (MB, IMAGE_TOKEN_ROWS, MODEL_WIDTH), 1.0, 6.0, ((0, 4), (1, 8), (2, 8)))
    in_gain = jnp.clip(1.0 + 0.15 * jax.random.normal(streams_of[4], (N_SECTION, MODEL_WIDTH), jnp.float32), 0.25, 1.75)
    wq = gaussian(streams_of[5], (N_SECTION, MODEL_WIDTH, QUERY_HEADS * HEAD_SIZE), MODEL_WIDTH ** -0.5, 0.0625, ((0, 8), (1, 4), (2, 8)))
    wk = gaussian(streams_of[6], (N_SECTION, MODEL_WIDTH, KEY_VALUE_HEADS * HEAD_SIZE), MODEL_WIDTH ** -0.5, 0.0625, ((0, 8), (1, 4), (2, 8)))
    wv = gaussian(streams_of[7], (N_SECTION, MODEL_WIDTH, KEY_VALUE_HEADS * HEAD_SIZE), MODEL_WIDTH ** -0.5, 0.0625, ((0, 8), (1, 4), (2, 8)))
    wo = gaussian(streams_of[8], (N_SECTION, QUERY_HEADS * HEAD_SIZE, MODEL_WIDTH), (QUERY_HEADS * HEAD_SIZE) ** -0.5, 0.09375, ((0, 8), (1, 8), (2, 4)))
    query_norm_gain = draw_query_norm_gain(jax.random.fold_in(streams_of[13], 71), 0)
    k_gain = draw_k_gain(jax.random.fold_in(streams_of[13], 71), 0)
    gate = jnp.clip(jax.random.uniform(streams_of[11], (N_SECTION,), jnp.float32, -1.5, 1.5) * shard_levels(streams_of[11], (N_SECTION,), ((0, 8),), -0.4, 0.0), -1.5, 1.5)
    cot = gaussian(streams_of[12], (N_SECTION, MB, TEXT_ROWS, MODEL_WIDTH), 1.0, 6.0, ((0, 8), (1, 4)))
    return dict(text=text, order=order, lengths=lengths, image=image, in_gain=in_gain, wq=wq, wk=wk, wv=wv, wo=wo, query_norm_gain=query_norm_gain, k_gain=k_gain, gate=gate, cot=cot)


EPS = 1e-05
HIGH = lax.Precision.HIGHEST

def root_mean_norm(value_rows, gain):
    return value_rows * lax.rsqrt(lax.optimization_barrier(jnp.mean(value_rows * value_rows, axis=-1, keepdims=True)) + EPS) * gain

def attend(queries, keys, value_rows):
    scores = jnp.einsum('brhgd,bkhd->bhgrk', queries, keys, precision=HIGH)
    probs = jax.nn.softmax(scores, axis=-1)
    return jnp.einsum('bhgrk,bkhd->brhgd', probs, value_rows, precision=HIGH)

def reference(text, order, lengths, image, in_gain, wq, wk, wv, wo, query_norm_gain, k_gain, gate, cot):
    query_group = QUERY_HEADS // KEY_VALUE_HEADS
    tally_count = N_DP * MB_DEV
    slice_width = QUERY_HEADS * HEAD_SIZE // N_TENSOR
    mb_ids = (jnp.arange(N_DP, dtype=jnp.int32)[:, None] * MB_DEV + order).reshape(-1)
    hidden = text[mb_ids]
    lens = lengths.reshape(-1)[mb_ids]
    valid_mask = (jnp.arange(TEXT_ROWS, dtype=jnp.int32)[None, :] < lens[:, None]).astype(jnp.float32)[:, :, None]
    flattened_image = image[mb_ids].reshape(tally_count * IMAGE_TOKEN_ROWS, MODEL_WIDTH)
    grad = jnp.zeros((tally_count * IMAGE_TOKEN_ROWS, MODEL_WIDTH), jnp.float32)
    outputs = []
    for layer_number in range(N_SECTION):
        hf = hidden.astype(jnp.float32)
        normed = root_mean_norm(hf, in_gain[layer_number]).astype(jnp.bfloat16)
        query_matrix = jnp.dot(normed.reshape(tally_count * TEXT_ROWS, MODEL_WIDTH), wq[layer_number], preferred_element_type=jnp.float32)
        query_matrix = root_mean_norm(query_matrix.reshape(tally_count, TEXT_ROWS, KEY_VALUE_HEADS, query_group, HEAD_SIZE), query_norm_gain[layer_number]) / math.sqrt(HEAD_SIZE)
        unnormed_key = jnp.dot(flattened_image, wk[layer_number], preferred_element_type=jnp.float32).reshape(tally_count, IMAGE_TOKEN_ROWS, KEY_VALUE_HEADS, HEAD_SIZE)
        k_normed = root_mean_norm(unnormed_key, k_gain[layer_number])
        value_rows = jnp.dot(flattened_image, wv[layer_number], preferred_element_type=jnp.float32).reshape(tally_count, IMAGE_TOKEN_ROWS, KEY_VALUE_HEADS, HEAD_SIZE)

        def attn_of(keys, vals):
            return attend(query_matrix, keys, vals)
        attended, pull = jax.vjp(attn_of, k_normed, value_rows)
        att16 = attended.astype(jnp.bfloat16).reshape(tally_count * TEXT_ROWS, QUERY_HEADS * HEAD_SIZE)
        out = jnp.zeros((tally_count * TEXT_ROWS, MODEL_WIDTH), jnp.float32)
        for part in range(N_TENSOR):
            lo = part * slice_width
            term = jnp.dot(att16[:, lo:lo + slice_width], wo[layer_number, lo:lo + slice_width], preferred_element_type=jnp.float32).astype(jnp.bfloat16)
            out = out + lax.optimization_barrier(term).astype(jnp.float32)
        logit_scale = jnp.tanh(gate[layer_number])
        hidden = (hf + logit_scale * valid_mask * out.reshape(tally_count, TEXT_ROWS, MODEL_WIDTH)).astype(jnp.bfloat16)
        outputs.append(hidden)
        backward_pass = jnp.dot(cot[layer_number].reshape(tally_count * TEXT_ROWS, MODEL_WIDTH), wo[layer_number].T, preferred_element_type=jnp.float32)
        attention_gradient = (logit_scale * valid_mask * backward_pass.reshape(tally_count, TEXT_ROWS, QUERY_HEADS * HEAD_SIZE)).reshape(tally_count, TEXT_ROWS, KEY_VALUE_HEADS, query_group, HEAD_SIZE)
        d_kn, value_gradient = pull(attention_gradient)
        kgain = k_gain[layer_number]
        _, norm_pull = jax.vjp(lambda keys: root_mean_norm(keys, kgain), unnormed_key)
        key_gradient = norm_pull(d_kn)[0]
        key_gradient_16 = key_gradient.astype(jnp.bfloat16).reshape(tally_count * IMAGE_TOKEN_ROWS, KEY_VALUE_HEADS * HEAD_SIZE)
        value_gradient_16 = value_gradient.astype(jnp.bfloat16).reshape(tally_count * IMAGE_TOKEN_ROWS, KEY_VALUE_HEADS * HEAD_SIZE)
        dims = (((1,), (1,)), ((), ()))
        grad = grad + lax.dot_general(key_gradient_16, wk[layer_number], dims, preferred_element_type=jnp.float32)
        grad = grad + lax.dot_general(value_gradient_16, wv[layer_number], dims, preferred_element_type=jnp.float32)
    states = jnp.stack(outputs)
    image_grad = jnp.zeros((tally_count, IMAGE_TOKEN_ROWS, MODEL_WIDTH), jnp.float32).at[mb_ids].set(grad.reshape(tally_count, IMAGE_TOKEN_ROWS, MODEL_WIDTH))
    return (states, image_grad)
```

```python
import functools
import math

import jax
import jax.numpy as jnp
from jax import lax
from jax.experimental import pallas as pl
from jax.experimental.pallas import tpu as pltpu
from jax.sharding import PartitionSpec as P

EPS = 1e-05
HIGH = lax.Precision.HIGHEST
LANES = 128
ROWS_ROWS = (((1,), (1,)), ((), ()))
COLS_COLS = (((0,), (0,)), ((), ()))


def dot32(a, b, dims=(((1,), (0,)), ((), ()))):
    return lax.dot_general(a, b, dims, precision=HIGH, preferred_element_type=jnp.float32)


def dot16(a, b, dims=(((1,), (0,)), ((), ()))):
    return lax.dot_general(a, b, dims, preferred_element_type=jnp.float32)


def front_kernel(first, last, n, ints, floats, *refs):
    refs = list(refs)
    text_ref = refs.pop(0)
    gain_ref = refs.pop(0)
    if not first:
        p_refs = [refs.pop(0) for _ in range(n)]
        vo_ref, h_ref = refs.pop(0), refs.pop(0)
    if not last:
        w_refs = [refs.pop(0) for _ in range(4)]
        q_ref = refs.pop(0)
        hq_ref = refs.pop(0)
    if not first:
        new_ref = refs.pop(0)
    if not last:
        x_s, ss_s = refs

    def head():
        if first:
            h = text_ref[0]
        else:
            probs = jnp.concatenate([r[...] for r in p_refs], axis=1)
            out = dot16(probs, vo_ref[0])
            row = lax.broadcasted_iota(jnp.int32, out.shape, 0)
            scale = jnp.where(row < ints[2], floats[0], 0.0)
            new = (h_ref[...].astype(jnp.float32) + scale * out).astype(jnp.bfloat16)
            new_ref[...] = new
            if last:
                return
            h = jnp.where(ints[3] > 0, text_ref[0], new)
        hq_ref[...] = h
        hf = h.astype(jnp.float32)
        x_s[...] = (hf * gain_ref[...]).astype(jnp.bfloat16)
        ss = jnp.sum(hf * hf, axis=1, keepdims=True)
        hi = ss.astype(jnp.bfloat16).astype(jnp.float32)
        lane = lax.broadcasted_iota(jnp.int32, ss_s.shape, 1)
        ss_s[...] = jnp.where(lane == 0, hi, ss - hi).astype(jnp.bfloat16)

    if last:
        head()
        return
    pl.when(pl.program_id(0) == 0)(head)
    chunk = w_refs[0].shape[1]
    acc = dot16(x_s[:, :chunk], w_refs[0][0])
    for j in range(1, 4):
        acc += dot16(x_s[:, j * chunk : (j + 1) * chunk], w_refs[j][0])
    cols = acc.shape[1]
    q_ref[0, :, :cols] = acc.astype(jnp.bfloat16)
    q_ref[0, :, cols:] = ss_s[...]


def front(ints, floats, text, gain, probs, vo, h, w, last=False):
    first = probs is None
    rows, feats = text.shape[1:]
    n = w[0].shape[0]
    cols = w[0].shape[2]
    chunk = w[0].shape[1]
    whole = lambda shape: pl.BlockSpec(shape, lambda k, *_: (0,) * len(shape))
    in_specs = [
        pl.BlockSpec(memory_space=pltpu.SMEM),
        pl.BlockSpec((1, rows, feats), lambda k, i: (i[1], 0, 0)),
        whole((1, feats)),
    ]
    args = [floats, text, gain]
    if not first:
        in_specs += [whole(p.shape) for p in probs]
        in_specs += [pl.BlockSpec((1,) + vo.shape[1:], lambda k, i: (i[0], 0, 0)), whole(h.shape)]
        args += list(probs) + [vo, h]
    outs, out_specs, scratch = [], [], []
    if not last:
        in_specs += [pl.BlockSpec((1, chunk, cols), lambda k, i: (k, 0, 0))] * 4
        args += list(w)
        outs += [
            jax.ShapeDtypeStruct((n, rows, cols + LANES), jnp.bfloat16),
            jax.ShapeDtypeStruct((rows, feats), jnp.bfloat16),
        ]
        out_specs += [
            pl.BlockSpec((1, rows, cols + LANES), lambda k, i: (k, 0, 0)),
            whole((rows, feats)),
        ]
        scratch = [pltpu.VMEM((rows, feats), jnp.bfloat16), pltpu.VMEM((rows, LANES), jnp.bfloat16)]
    if not first:
        outs.append(jax.ShapeDtypeStruct((rows, feats), jnp.bfloat16))
        out_specs.append(whole((rows, feats)))
    return pl.pallas_call(
        functools.partial(front_kernel, first, last, n),
        grid_spec=pltpu.PrefetchScalarGridSpec(
            num_scalar_prefetch=1,
            grid=(1 if last else n,),
            in_specs=in_specs,
            out_specs=out_specs,
            scratch_shapes=scratch,
        ),
        out_shape=outs,
        compiler_params=pltpu.CompilerParams(vmem_limit_bytes=32 * 2**20),
    )(ints, *args)


def attend_kernel(n, width, ints, gain_ref, k_ref, own_ref, *refs):
    others, p_ref, qn_ref = refs[: n - 1], refs[n - 1], refs[n]
    total = own_ref[0].astype(jnp.float32)
    for r in others:
        total += r[...].astype(jnp.float32)
    hd = gain_ref.shape[1]
    cols = qn_ref.shape[1]
    ss = total[:, cols : cols + 1] + total[:, cols + 1 : cols + 2]
    rs = lax.rsqrt(ss / width + EPS)
    keys = k_ref[0]
    parts = []
    for h in range(cols // hd):
        q = total[:, h * hd : (h + 1) * hd] * rs
        r = lax.rsqrt(jnp.mean(q * q, axis=1, keepdims=True) + EPS)
        qn = q * r * gain_ref[...] * (1.0 / math.sqrt(hd))
        qn_ref[:, h * hd : (h + 1) * hd] = qn
        sc = dot32(qn, keys, ROWS_ROWS)
        e = jnp.exp(sc - jnp.max(sc, axis=1, keepdims=True))
        parts.append(e / jnp.sum(e, axis=1, keepdims=True))
    p_ref[...] = jnp.concatenate(parts, axis=1).astype(jnp.bfloat16)


def attend(ints, width, gain, keys, own, others):
    n, rows, wide = own.shape
    cols = wide - LANES
    hd = gain.shape[1]
    toks = keys.shape[1]
    whole = lambda shape: pl.BlockSpec(shape, lambda k, *_: (0,) * len(shape))
    return pl.pallas_call(
        functools.partial(attend_kernel, n, width),
        grid_spec=pltpu.PrefetchScalarGridSpec(
            num_scalar_prefetch=1,
            grid=(1,),
            in_specs=[
                whole(gain.shape),
                pl.BlockSpec((1,) + keys.shape[1:], lambda k, i: (i[1], 0, 0)),
                whole((1, rows, wide)),
            ]
            + [whole((rows, wide))] * (n - 1),
            out_specs=[whole((rows, cols // hd * toks)), whole((rows, cols))],
        ),
        out_shape=[
            jax.ShapeDtypeStruct((rows, cols // hd * toks), jnp.bfloat16),
            jax.ShapeDtypeStruct((rows, cols), jnp.float32),
        ],
    )(ints, gain, keys, own, *others)


def value_out_kernel(slots, v_ref, *refs):
    w_refs, o_ref = refs[:4], refs[4]
    v = v_ref[0]
    hd = v.shape[1]
    toks = v.shape[0] // slots
    chunk = w_refs[0].shape[2]
    for h in range(w_refs[0].shape[1] // hd):
        for j in range(4):
            r = dot16(v, w_refs[j][0, h * hd : (h + 1) * hd, :]).astype(jnp.bfloat16)
            for o in range(slots):
                o_ref[o, h * toks : (h + 1) * toks, j * chunk : (j + 1) * chunk] = r[
                    o * toks : (o + 1) * toks
                ]


def value_out(v, w, slots):
    n, vrows, hd = v.shape
    heads = w[0].shape[1] // hd
    chunk = w[0].shape[2]
    toks = vrows // slots
    return pl.pallas_call(
        functools.partial(value_out_kernel, slots),
        grid=(n,),
        in_specs=[pl.BlockSpec((1, vrows, hd), lambda k: (k, 0, 0))]
        + [pl.BlockSpec((1,) + w[0].shape[1:], lambda k: (k, 0, 0))] * 4,
        out_specs=pl.BlockSpec((slots, heads * toks, 4 * chunk), lambda k: (0, k, 0)),
        out_shape=jax.ShapeDtypeStruct((slots, n * heads * toks, 4 * chunk), jnp.bfloat16),
        compiler_params=pltpu.CompilerParams(vmem_limit_bytes=32 * 2**20),
    )(v, *w)


def back_kernel(qn_ref, k_ref, v_ref, raw_ref, da_ref, gain_ref, o_ref):
    keys, vals, raw, gain = k_ref[0], v_ref[0], raw_ref[0], gain_ref[...]
    hd = keys.shape[1]
    d_kn = jnp.zeros(keys.shape, jnp.float32)
    d_v = jnp.zeros(keys.shape, jnp.float32)
    for h in range(qn_ref.shape[2] // hd):
        qn = qn_ref[0, :, h * hd : (h + 1) * hd]
        da = da_ref[0, :, h * hd : (h + 1) * hd]
        sc = dot32(qn, keys, ROWS_ROWS)
        e = jnp.exp(sc - jnp.max(sc, axis=1, keepdims=True))
        p = e / jnp.sum(e, axis=1, keepdims=True)
        dp = dot32(da, vals, ROWS_ROWS)
        ds = p * (dp - jnp.sum(p * dp, axis=1, keepdims=True))
        d_kn += dot32(ds, qn, COLS_COLS)
        d_v += dot32(p, da, COLS_COLS)
    r = lax.rsqrt(jnp.mean(raw * raw, axis=1, keepdims=True) + EPS)
    u = d_kn * gain
    d_k = r * u - raw * (r * r * r * jnp.mean(raw * u, axis=1, keepdims=True))
    o_ref[0, :, :hd] = d_k.astype(jnp.bfloat16)
    o_ref[0, :, hd:] = d_v.astype(jnp.bfloat16)


def back(qn, keys, vals, raw, da, gain):
    slots, toks, hd = keys.shape
    one = lambda a: pl.BlockSpec((1,) + a.shape[1:], lambda o: (o, 0, 0))
    return pl.pallas_call(
        back_kernel,
        grid=(slots,),
        in_specs=[one(qn), one(keys), one(vals), one(raw), one(da), pl.BlockSpec(gain.shape, lambda o: (0, 0))],
        out_specs=pl.BlockSpec((1, toks, 2 * hd), lambda o: (o, 0, 0)),
        out_shape=jax.ShapeDtypeStruct((slots, toks, 2 * hd), jnp.bfloat16),
    )(qn, keys, vals, raw, da, gain)


def pick(a, i, axis=0):
    return lax.dynamic_index_in_dim(a, i, axis, keepdims=False)


def per_device(
    text, order, lengths, image, in_gain, wq, wk, wv, wo, query_norm_gain, k_gain, gate, cot
):
    D, S, T = lax.axis_size("dp"), lax.axis_size("section"), lax.axis_size("tensor")
    R = T // D
    d, s, t = lax.axis_index("dp"), lax.axis_index("section"), lax.axis_index("tensor")
    slots, rows = text.shape[:2]
    width = in_gain.shape[1]
    hd = k_gain.shape[1]
    feats = width // T
    chunk = feats // D
    toks = image.shape[1] * S

    def along(x, k):
        return lax.ppermute(x, "tensor", [(i, (i + k) % T) for i in range(T)]) if k % T else x

    def onward(x, k):
        pairs = [(a * T + i, (a + 1) % S * T + (i + k) % T) for a in range(S) for i in range(T)]
        return lax.ppermute(x, ("section", "tensor"), pairs)

    def dp_flip(x, m):
        return lax.ppermute(x, "dp", [(i, i ^ m) for i in range(D)])

    def dp_all(x):
        across = dp_flip(x, 2)
        return [x, dp_flip(x, 1), across, dp_flip(across, 1)]

    def spread(x):
        a, c = t // R, t % D
        parts = jnp.stack(jnp.split(x, D, axis=-1))
        got = []
        for k in range(D):
            pairs = [(i * R + b, b * D + (i + k) % D) for i in range(D) for b in range(R)]
            got.append(lax.ppermute(pick(parts, (a + k) % D), "tensor", pairs))
        got = jnp.stack(got)
        return jnp.concatenate([pick(got, (c - (d ^ j)) % D) for j in range(D)], axis=-1)

    def unspread(x, back_sections):
        a, c = t // R, t % D
        parts = jnp.stack(jnp.split(x, D, axis=-1))
        got = []
        for k in range(D):
            pairs = [
                (e * T + b * D + (i + k) % D, (e - back_sections) % S * T + i * R + b)
                for e in range(S)
                for i in range(D)
                for b in range(R)
            ]
            got.append(lax.ppermute(pick(parts, ((c - k) % D) ^ d), ("section", "tensor"), pairs))
        got = jnp.stack(got)
        return jnp.concatenate([pick(got, (j - a) % D) for j in range(D)], axis=-1)

    micro = order[0]
    lens = jnp.take(lengths[0], micro)
    text_f = spread(jnp.take(text, micro, axis=0))
    img = spread(jnp.take(image, micro, axis=0))
    img = jnp.stack(
        [img]
        + [
            lax.ppermute(img, "section", [(i, (i + k) % S) for i in range(S)])
            for k in range(1, S)
        ],
        axis=1,
    ).reshape(slots * toks, feats)
    gain_f = pick(in_gain.reshape(D, T, chunk), t, 1)
    gain_f = jnp.concatenate([pick(gain_f, d ^ j) for j in range(D)])[None]

    def by_features(w):
        pieces = w.reshape(T, chunk, w.shape[1])
        return dp_all(jnp.stack([along(pick(pieces, (t + k) % T), k) for k in range(T)]))

    wkv_f = by_features(jnp.concatenate([wk[0], wv[0]], axis=1))
    wq_f = by_features(wq[0])
    pieces = wo[0].reshape(wo.shape[1], T, chunk)
    wo_f = dp_all(jnp.stack([onward(pick(pieces, (t + k) % T, 1), k) for k in range(T)]))
    wo_full = lax.all_gather(wo[0], "dp", axis=1, tiled=True)

    kv = sum(
        jnp.einsum(
            "rf,kfc->krc", img[:, j * chunk : (j + 1) * chunk], wkv_f[j],
            preferred_element_type=jnp.float32,
        )
        for j in range(D)
    ).astype(jnp.bfloat16)
    kv = sum(along(kv[k], -k).astype(jnp.float32) for k in range(T)).reshape(slots, toks, 2 * hd)
    k_raw, vals = kv[..., :hd], kv[..., hd:]
    keys = k_raw * lax.rsqrt(jnp.mean(k_raw * k_raw, axis=-1, keepdims=True) + EPS) * k_gain[0]
    vals16 = vals.astype(jnp.bfloat16).reshape(slots * toks, hd)
    vo = value_out(jnp.stack([onward(vals16, k) for k in range(T)]), wo_f, slots)

    alpha = jnp.tanh(gate)
    alpha_before = lax.ppermute(alpha, "section", [(i, (i + 1) % S) for i in range(S)])

    probs = h = None
    all_qn, all_h = [], []
    for step in range(S + slots):
        slot_in = jnp.clip(step - s, 0, slots - 1)
        slot_out = jnp.clip(jnp.where(s == 0, step - S, step - s), 0, slots - 1)
        ints = jnp.stack([slot_out, slot_in, lens[slot_out], (s == 0).astype(jnp.int32)])
        last = step == S + slots - 1
        got = front(ints, alpha_before, text_f, gain_f, probs, vo, h, wq_f, last)
        if step > 0:
            all_h.append(got[-1])
        if last:
            break
        parts, hq = got[:2]
        others = [along(parts[k], -k) for k in range(1, T)]
        p, qn = attend(ints, width, query_norm_gain, keys, parts, others)
        all_qn.append(qn)
        probs = [onward(p, k) for k in range(T)]
        h = onward(hq, 0)

    states = lax.dynamic_slice_in_dim(jnp.stack(all_h), (s - 1) % S, slots, 0)
    states = unspread(states, 1)

    qn = lax.dynamic_slice_in_dim(jnp.stack(all_qn), s, slots, 0)
    mask = (jnp.arange(rows)[None, :] < lens[:, None]).astype(jnp.float32)[:, :, None]
    d_attn = dot16(cot[0].reshape(slots * rows, width), wo_full, ROWS_ROWS)
    d_attn = alpha[0] * mask * d_attn.reshape(slots, rows, -1)
    d_kv = back(qn, keys, vals, k_raw, d_attn, k_gain).reshape(slots * toks, 2 * hd)
    d_kv = jnp.stack([along(d_kv, k) for k in range(T)])
    grad = jnp.concatenate(
        [
            jnp.einsum("krc,kfc->rf", d_kv, wkv_f[j], preferred_element_type=jnp.float32)
            for j in range(D)
        ],
        axis=1,
    )
    grad = grad.astype(jnp.bfloat16).reshape(slots, S, toks // S, feats)
    grad = grad[:, 0].astype(jnp.float32) + sum(
        lax.ppermute(grad[:, k], "section", [(i, (i - k) % S) for i in range(S)]).astype(jnp.float32)
        for k in range(1, S)
    )
    grad = unspread(grad, 0)
    grad = jnp.stack([pick(grad, jnp.argmax(micro == m)) for m in range(slots)])
    return (states[None], grad)


def solution(mesh):
    return jax.shard_map(
        per_device,
        mesh=mesh,
        in_specs=(
            P("dp", None, "tensor"),
            P("dp", None),
            P("dp", None),
            P("dp", "section", "tensor"),
            P("section", None),
            P("section", "dp", "tensor"),
            P("section", "dp", "tensor"),
            P("section", "dp", "tensor"),
            P("section", "tensor", "dp"),
            P("section", None),
            P("section", None),
            P("section"),
            P("section", "dp", None, None),
        ),
        out_specs=(P("section", "dp", None, "tensor"), P("dp", "section", "tensor")),
        check_vma=False,
    )
```

```python
import functools
import math

import jax
import jax.numpy as jnp
from jax import lax
from jax.experimental import pallas as pl
from jax.experimental.pallas import tpu as pltpu
from jax.sharding import PartitionSpec as P

EPS = 1e-05
HIGH = lax.Precision.HIGHEST
LANES = 128
EXTRA = 16
VMEM_BYTES = 56 * 2**20
ROWS_ROWS = (((1,), (1,)), ((), ()))
COLS_COLS = (((0,), (0,)), ((), ()))


def dot32(a, b, dims=(((1,), (0,)), ((), ()))):
    return lax.dot_general(a, b, dims, precision=HIGH, preferred_element_type=jnp.float32)


def dot16(a, b, dims=(((1,), (0,)), ((), ()))):
    return lax.dot_general(a, b, dims, preferred_element_type=jnp.float32)


def front_kernel(first, last, ints, *refs):
    refs = list(refs)
    text_ref, gain_ref = refs.pop(0), refs.pop(0)
    if not first:
        p_ref, vo_ref, h_ref = refs.pop(0), refs.pop(0), refs.pop(0)
    if not last:
        w_refs = [refs.pop(0) for _ in range(4)]
        q_ref, hq_ref = refs.pop(0), refs.pop(0)
    if not first:
        new_ref = refs.pop(0)
    if not last:
        x_s, ss_s = refs

    def head():
        if first:
            h = text_ref[0]
        else:
            probs = jnp.concatenate([p_ref[i] for i in range(p_ref.shape[0])], axis=1)
            out = dot16(probs, vo_ref[0])
            new = (h_ref[...].astype(jnp.float32) + out).astype(jnp.bfloat16)
            new_ref[...] = new
            if last:
                return
            h = jnp.where(ints[3] > 0, text_ref[0], new)
        hq_ref[...] = h
        hf = h.astype(jnp.float32)
        x_s[...] = (hf * gain_ref[...]).astype(jnp.bfloat16)
        ss = jnp.sum(hf * hf, axis=1, keepdims=True)
        hi = ss.astype(jnp.bfloat16).astype(jnp.float32)
        own, lane = own_lanes(h.shape[0])
        pair = jnp.where(lane < h.shape[0], hi, ss - hi)
        pair = jnp.sum(jnp.where(own, pair, 0.0), axis=0, keepdims=True)
        ss_s[...] = jnp.broadcast_to(pair, ss_s.shape).astype(jnp.bfloat16)

    if last:
        head()
        return
    pl.when(pl.program_id(0) == 0)(head)
    chunk = w_refs[0].shape[1]
    acc = dot16(x_s[:, :chunk], w_refs[0][0])
    for j in range(1, 4):
        acc += dot16(x_s[:, j * chunk : (j + 1) * chunk], w_refs[j][0])
    acc = acc.astype(jnp.bfloat16)
    rows = acc.shape[0]
    for i in range(acc.shape[1] // LANES):
        q_ref[0, i * rows : (i + 1) * rows, :] = acc[:, i * LANES : (i + 1) * LANES]
    q_ref[0, -EXTRA:, :] = ss_s[...]


def own_lanes(rows):
    row = lax.broadcasted_iota(jnp.int32, (rows, LANES), 0)
    lane = lax.broadcasted_iota(jnp.int32, (rows, LANES), 1)
    return (lane == row) | (lane == row + rows), lane


def whole(shape):
    return pl.BlockSpec(shape, lambda *_: (0,) * len(shape))


def front(ints, text, gain, probs, vo, h, w, last=False):
    first = probs is None
    rows, feats = text.shape[1:]
    n, chunk, cols = w[0].shape
    in_specs = [pl.BlockSpec((1, rows, feats), lambda k, i: (i[1], 0, 0)), whole((1, feats))]
    args = [text, gain]
    if not first:
        in_specs += [
            whole(probs.shape),
            pl.BlockSpec((1,) + vo.shape[1:], lambda k, i: (i[0], 0, 0)),
            whole(h.shape),
        ]
        args += [probs, vo, h]
    outs, out_specs, scratch = [], [], []
    state = jax.ShapeDtypeStruct((rows, feats), jnp.bfloat16)
    if not last:
        in_specs += [pl.BlockSpec((1, chunk, cols), lambda k, i: (k, 0, 0))] * 4
        args += list(w)
        part = (cols // LANES * rows + EXTRA, LANES)
        outs += [jax.ShapeDtypeStruct((n,) + part, jnp.bfloat16), state]
        out_specs += [pl.BlockSpec((1,) + part, lambda k, i: (k, 0, 0)), whole((rows, feats))]
        scratch = [pltpu.VMEM((rows, feats), jnp.bfloat16), pltpu.VMEM((EXTRA, LANES), jnp.bfloat16)]
    if not first:
        outs.append(state)
        out_specs.append(whole((rows, feats)))
    return pl.pallas_call(
        functools.partial(front_kernel, first, last),
        grid_spec=pltpu.PrefetchScalarGridSpec(
            num_scalar_prefetch=1,
            grid=(1 if last else n,),
            in_specs=in_specs,
            out_specs=out_specs,
            scratch_shapes=scratch,
        ),
        out_shape=outs,
        compiler_params=pltpu.CompilerParams(vmem_limit_bytes=VMEM_BYTES),
    )(ints, *args)


def attend_kernel(width, ints, alpha_ref, gain_ref, k_ref, q_ref, p_ref, qn_ref):
    total = q_ref[0].astype(jnp.float32)
    for i in range(1, q_ref.shape[0]):
        total += q_ref[i].astype(jnp.float32)
    hd = gain_ref.shape[1]
    rows, cols = qn_ref.shape
    own, _ = own_lanes(rows)
    sums = jnp.broadcast_to(total[cols // hd * rows : cols // hd * rows + 1], (rows, LANES))
    ss = jnp.sum(jnp.where(own, sums, 0.0), axis=1, keepdims=True)
    rs = lax.rsqrt(ss / width + EPS)
    keys = k_ref[0]
    row = lax.broadcasted_iota(jnp.int32, (rows, keys.shape[0]), 0)
    scale = jnp.where(row < ints[2], alpha_ref[0], 0.0)
    parts = []
    for h in range(cols // hd):
        q = total[h * rows : (h + 1) * rows] * rs
        r = lax.rsqrt(jnp.mean(q * q, axis=1, keepdims=True) + EPS)
        qn = q * r * gain_ref[...] * (1.0 / math.sqrt(hd))
        qn_ref[:, h * hd : (h + 1) * hd] = qn
        sc = dot32(qn, keys, ROWS_ROWS)
        e = jnp.exp(sc - jnp.max(sc, axis=1, keepdims=True))
        parts.append(scale * e / jnp.sum(e, axis=1, keepdims=True))
    p_ref[...] = jnp.concatenate(parts, axis=1).astype(jnp.bfloat16)


def attend(ints, alpha, width, gain, keys, parts):
    hd = gain.shape[1]
    toks = keys.shape[1]
    heads = 4
    rows = (parts.shape[1] - EXTRA) // heads
    return pl.pallas_call(
        functools.partial(attend_kernel, width),
        grid_spec=pltpu.PrefetchScalarGridSpec(
            num_scalar_prefetch=1,
            grid=(1,),
            in_specs=[
                pl.BlockSpec(memory_space=pltpu.SMEM),
                whole(gain.shape),
                pl.BlockSpec((1,) + keys.shape[1:], lambda k, i: (i[1], 0, 0)),
                whole(parts.shape),
            ],
            out_specs=[whole((rows, heads * toks)), whole((rows, heads * hd))],
        ),
        out_shape=[
            jax.ShapeDtypeStruct((rows, heads * toks), jnp.bfloat16),
            jax.ShapeDtypeStruct((rows, heads * hd), jnp.float32),
        ],
    )(ints, alpha, gain, keys, parts)


def value_out_kernel(slots, v_ref, *refs):
    w_refs, o_ref = refs[:4], refs[4]
    v = v_ref[0]
    hd = v.shape[1]
    toks = v.shape[0] // slots
    chunk = w_refs[0].shape[2]
    for h in range(w_refs[0].shape[1] // hd):
        for j in range(4):
            r = dot16(v, w_refs[j][0, h * hd : (h + 1) * hd, :]).astype(jnp.bfloat16)
            for o in range(slots):
                o_ref[o, h * toks : (h + 1) * toks, j * chunk : (j + 1) * chunk] = r[
                    o * toks : (o + 1) * toks
                ]


def value_out(v, w, slots):
    n, vrows, hd = v.shape
    heads = w[0].shape[1] // hd
    chunk = w[0].shape[2]
    toks = vrows // slots
    return pl.pallas_call(
        functools.partial(value_out_kernel, slots),
        grid=(n,),
        in_specs=[pl.BlockSpec((1, vrows, hd), lambda k: (k, 0, 0))]
        + [pl.BlockSpec((1,) + w[0].shape[1:], lambda k: (k, 0, 0))] * 4,
        out_specs=pl.BlockSpec((slots, heads * toks, 4 * chunk), lambda k: (0, k, 0)),
        out_shape=jax.ShapeDtypeStruct((slots, n * heads * toks, 4 * chunk), jnp.bfloat16),
        compiler_params=pltpu.CompilerParams(vmem_limit_bytes=VMEM_BYTES),
    )(v, *w)


def back_kernel(qn_ref, k_ref, v_ref, raw_ref, da_ref, gain_ref, o_ref):
    keys, vals, raw, gain = k_ref[0], v_ref[0], raw_ref[0], gain_ref[...]
    hd = keys.shape[1]
    d_kn = jnp.zeros(keys.shape, jnp.float32)
    d_v = jnp.zeros(keys.shape, jnp.float32)
    for h in range(qn_ref.shape[2] // hd):
        qn = qn_ref[0, :, h * hd : (h + 1) * hd]
        da = da_ref[0, :, h * hd : (h + 1) * hd]
        sc = dot32(qn, keys, ROWS_ROWS)
        e = jnp.exp(sc - jnp.max(sc, axis=1, keepdims=True))
        p = e / jnp.sum(e, axis=1, keepdims=True)
        dp = dot32(da, vals, ROWS_ROWS)
        ds = p * (dp - jnp.sum(p * dp, axis=1, keepdims=True))
        d_kn += dot32(ds, qn, COLS_COLS)
        d_v += dot32(p, da, COLS_COLS)
    r = lax.rsqrt(jnp.mean(raw * raw, axis=1, keepdims=True) + EPS)
    u = d_kn * gain
    d_k = r * u - raw * (r * r * r * jnp.mean(raw * u, axis=1, keepdims=True))
    o_ref[0, :, :hd] = d_k.astype(jnp.bfloat16)
    o_ref[0, :, hd:] = d_v.astype(jnp.bfloat16)


def back(qn, keys, vals, raw, da, gain):
    slots, toks, hd = keys.shape
    one = lambda a: pl.BlockSpec((1,) + a.shape[1:], lambda o: (o, 0, 0))
    return pl.pallas_call(
        back_kernel,
        grid=(slots,),
        in_specs=[one(qn), one(keys), one(vals), one(raw), one(da), pl.BlockSpec(gain.shape, lambda o: (0, 0))],
        out_specs=pl.BlockSpec((1, toks, 2 * hd), lambda o: (o, 0, 0)),
        out_shape=jax.ShapeDtypeStruct((slots, toks, 2 * hd), jnp.bfloat16),
    )(qn, keys, vals, raw, da, gain)


def pick(a, i, axis=0):
    return lax.dynamic_index_in_dim(a, i, axis, keepdims=False)


def after(x, *others):
    return lax.optimization_barrier((x,) + others)[0]


def swap(x, axis):
    return lax.all_to_all(x, axis, 0, 0, tiled=True)


def share(x, axis):
    return swap(jnp.broadcast_to(x[None], (lax.axis_size(axis),) + x.shape), axis)


def per_device(
    text, order, lengths, image, in_gain, wq, wk, wv, wo, query_norm_gain, k_gain, gate, cot
):
    D, S, T = lax.axis_size("dp"), lax.axis_size("section"), lax.axis_size("tensor")
    R = T // D
    d, s, t = lax.axis_index("dp"), lax.axis_index("section"), lax.axis_index("tensor")
    slots, rows = text.shape[:2]
    width = in_gain.shape[1]
    hd = k_gain.shape[1]
    feats = width // T
    chunk = feats // D
    toks = image.shape[1] * S

    def onward(x):
        return lax.ppermute(x, "section", [(i, (i + 1) % S) for i in range(S)])

    def dp_flip(x, m):
        return lax.ppermute(x, "dp", [(i, i ^ m) for i in range(D)])

    def dp_all(x):
        across = dp_flip(x, 2)
        return [x, dp_flip(x, 1), across, dp_flip(across, 1)]

    def spread(x):
        parts = jnp.stack(jnp.split(x, D, axis=-1))
        got = swap(jnp.concatenate([parts] * R), "tensor")
        got = pick(got.reshape((D, R) + got.shape[1:]), t // D, 1)
        return jnp.concatenate([pick(got, d ^ j) for j in range(D)], axis=-1)

    def unspread(x, back_sections):
        a, c = t // R, t % D
        parts = jnp.stack(jnp.split(x, D, axis=-1))
        got = []
        for k in range(D):
            pairs = [
                (e * T + b * D + (i + k) % D, (e - back_sections) % S * T + i * R + b)
                for e in range(S)
                for i in range(D)
                for b in range(R)
            ]
            got.append(lax.ppermute(pick(parts, ((c - k) % D) ^ d), ("section", "tensor"), pairs))
        got = jnp.stack(got)
        return jnp.concatenate([pick(got, (j - a) % D) for j in range(D)], axis=-1)

    micro = order[0]
    lens = jnp.take(lengths[0], micro)
    alpha = jnp.tanh(gate)

    img = jnp.moveaxis(share(jnp.take(image, micro, axis=0), "section"), 0, 1)
    img = lax.all_gather(img.reshape(slots * toks, feats), "tensor", axis=1, tiled=True)
    wkv = jnp.concatenate([wk[0], wv[0]], axis=1)
    wkv = lax.all_gather(wkv, "dp", axis=0, tiled=True)
    kv = jnp.dot(img, wkv, preferred_element_type=jnp.float32).reshape(slots, toks, 2 * hd)
    k_raw, vals = kv[..., :hd], kv[..., hd:]
    keys = k_raw * lax.rsqrt(jnp.mean(k_raw * k_raw, axis=-1, keepdims=True) + EPS) * k_gain[0]

    wo_next = onward(wo[0])
    wq_own = swap(wq[0].reshape(T, chunk, wq.shape[2]), "tensor")
    wq_f = dp_all(wq_own)
    text_f = after(jnp.take(text, micro, axis=0), wq_own)
    text_f = spread(text_f)
    gain_f = pick(in_gain.reshape(D, T, chunk), t, 1)
    gain_f = jnp.concatenate([pick(gain_f, d ^ j) for j in range(D)])[None]
    wo_own = jnp.moveaxis(wo_next.reshape(wo.shape[1], T, chunk), 1, 0)
    wo_own = swap(after(wo_own, text_f), "tensor")
    wo_f = dp_all(wo_own)

    probs = h = vo = None
    all_qn, all_h = [], []
    for step in range(S + slots):
        slot_in = jnp.clip(step - s, 0, slots - 1)
        slot_out = jnp.clip(jnp.where(s == 0, step - S, step - s), 0, slots - 1)
        ints = jnp.stack([slot_out, slot_in, lens[slot_in], (s == 0).astype(jnp.int32)])
        last = step == S + slots - 1
        got = front(ints, text_f, gain_f, probs, vo, h, wq_f, last)
        if step > 0:
            all_h.append(got[-1])
        if last:
            break
        parts, hq = got[:2]
        h = onward(hq)
        p, qn = attend(ints, alpha, width, query_norm_gain, keys, swap(parts, "tensor"))
        all_qn.append(qn)
        if step == 0:
            vals16 = vals.astype(jnp.bfloat16).reshape(slots * toks, hd)
            both = share(onward(jnp.concatenate([p, vals16])), "tensor")
            probs = both[:, :rows]
            vo = value_out(both[:, rows:], wo_f, slots)
        else:
            probs = share(onward(p), "tensor")
        if step == 1:
            wo_full = lax.all_gather(after(wo[0], p), "dp", axis=1, tiled=True)

    states = lax.dynamic_slice_in_dim(jnp.stack(all_h), (s - 1) % S, slots, 0)
    states = unspread(states, 1)

    qn = lax.dynamic_slice_in_dim(jnp.stack(all_qn), s, slots, 0)
    mask = (jnp.arange(rows)[None, :] < lens[:, None]).astype(jnp.float32)[:, :, None]
    d_attn = dot16(cot[0].reshape(slots * rows, width), wo_full, ROWS_ROWS)
    d_attn = alpha[0] * mask * d_attn.reshape(slots, rows, -1)
    d_kv = back(qn, keys, vals, k_raw, d_attn, k_gain).reshape(slots * toks, 2 * hd)
    grad = dot16(d_kv, wkv, ROWS_ROWS).astype(jnp.bfloat16)
    grad = swap(jnp.moveaxis(grad.reshape(slots * toks, T, feats), 1, 0), "tensor")
    grad = jnp.sum(grad.astype(jnp.float32), axis=0).astype(jnp.bfloat16)
    grad = swap(jnp.moveaxis(grad.reshape(slots, S, toks // S, feats), 1, 0), "section")
    grad = jnp.sum(grad.astype(jnp.float32), axis=0)
    grad = jnp.stack([pick(grad, jnp.argmax(micro == m)) for m in range(slots)])
    return (states[None], grad)


def solution(mesh):
    return jax.shard_map(
        per_device,
        mesh=mesh,
        in_specs=(
            P("dp", None, "tensor"),
            P("dp", None),
            P("dp", None),
            P("dp", "section", "tensor"),
            P("section", None),
            P("section", "dp", "tensor"),
            P("section", "dp", "tensor"),
            P("section", "dp", "tensor"),
            P("section", "tensor", "dp"),
            P("section", None),
            P("section", None),
            P("section"),
            P("section", "dp", None, None),
        ),
        out_specs=(P("section", "dp", None, "tensor"), P("dp", "section", "tensor")),
        check_vma=False,
    )
```

```python
import functools
import math

import jax
import jax.numpy as jnp
from jax import lax
from jax.experimental import pallas as pl
from jax.experimental.pallas import tpu as pltpu
from jax.sharding import PartitionSpec as P

EPS = 1e-05
HIGH = lax.Precision.HIGHEST
LANES = 128
EXTRA = 16
VMEM_BYTES = 24 * 2**20
ROWS_ROWS = (((1,), (1,)), ((), ()))
COLS_COLS = (((0,), (0,)), ((), ()))


def dot32(a, b, dims=(((1,), (0,)), ((), ()))):
    return lax.dot_general(a, b, dims, precision=HIGH, preferred_element_type=jnp.float32)


def dot16(a, b, dims=(((1,), (0,)), ((), ()))):
    return lax.dot_general(a, b, dims, preferred_element_type=jnp.float32)


def front_kernel(first, last, ints, *refs):
    refs = list(refs)
    text_ref, gain_ref = refs.pop(0), refs.pop(0)
    if not first:
        p_ref, vo_ref, h_ref = refs.pop(0), refs.pop(0), refs.pop(0)
    if not last:
        w_refs = [refs.pop(0) for _ in range(4)]
        q_ref, hq_ref = refs.pop(0), refs.pop(0)
    if not first:
        new_ref = refs.pop(0)
    if not last:
        x_s = refs.pop(0)

    if first:
        h = text_ref[ints[1]]
    else:
        probs = jnp.concatenate([p_ref[i] for i in range(p_ref.shape[0])], axis=1)
        new = h_ref[...].astype(jnp.float32) + dot16(probs, vo_ref[ints[0]])
        new = new.astype(jnp.bfloat16)
        new_ref[...] = new
        if last:
            return
        h = jnp.where(ints[3] > 0, text_ref[ints[1]], new)
    hq_ref[...] = h
    hf = h.astype(jnp.float32)
    x_s[...] = (hf * gain_ref[...]).astype(jnp.bfloat16)
    ss = jnp.sum(hf * hf, axis=1, keepdims=True)
    hi = ss.astype(jnp.bfloat16).astype(jnp.float32)
    rows = h.shape[0]
    own, lane = own_lanes(rows)
    pair = jnp.where(own, jnp.where(lane < rows, hi, ss - hi), 0.0)
    pair = jnp.broadcast_to(jnp.sum(pair, axis=0, keepdims=True), (EXTRA, LANES))
    pair = pair.astype(jnp.bfloat16)
    n, chunk, cols = w_refs[0].shape

    def block(k, carry):
        acc = dot16(x_s[:, :chunk], w_refs[0][k])
        for j in range(1, 4):
            acc += dot16(x_s[:, j * chunk : (j + 1) * chunk], w_refs[j][k])
        acc = acc.astype(jnp.bfloat16)
        for i in range(cols // LANES):
            q_ref[k, i * rows : (i + 1) * rows, :] = acc[:, i * LANES : (i + 1) * LANES]
        q_ref[k, cols // LANES * rows :, :] = pair
        return carry

    lax.fori_loop(0, n, block, 0)


def own_lanes(rows):
    row = lax.broadcasted_iota(jnp.int32, (rows, LANES), 0)
    lane = lax.broadcasted_iota(jnp.int32, (rows, LANES), 1)
    return (lane == row) | (lane == row + rows), lane


def whole(shape):
    return pl.BlockSpec(shape, lambda *_: (0,) * len(shape))


def front(ints, text, gain, probs, vo, h, w, last=False):
    first = probs is None
    rows, feats = text.shape[1:]
    n, _, cols = w[0].shape
    args = [text, gain]
    if not first:
        args += [probs, vo, h]
    outs, scratch = [], []
    state = jax.ShapeDtypeStruct((rows, feats), jnp.bfloat16)
    if not last:
        args += list(w)
        part = (cols // LANES * rows + EXTRA, LANES)
        outs += [jax.ShapeDtypeStruct((n,) + part, jnp.bfloat16), state]
        scratch = [pltpu.VMEM((rows, feats), jnp.bfloat16)]
    if not first:
        outs.append(state)
    return pl.pallas_call(
        functools.partial(front_kernel, first, last),
        in_specs=[pl.BlockSpec(memory_space=pltpu.SMEM)]
        + [pl.BlockSpec(memory_space=pltpu.VMEM)] * len(args),
        out_specs=[pl.BlockSpec(memory_space=pltpu.VMEM)] * len(outs),
        out_shape=outs,
        scratch_shapes=scratch,
        compiler_params=pltpu.CompilerParams(vmem_limit_bytes=VMEM_BYTES),
    )(ints, *args)


def attend_kernel(width, ints, alpha_ref, gain_ref, k_ref, q_ref, p_ref, qn_ref):
    total = q_ref[0].astype(jnp.float32)
    for i in range(1, q_ref.shape[0]):
        total += q_ref[i].astype(jnp.float32)
    hd = gain_ref.shape[1]
    rows, cols = qn_ref.shape
    own, _ = own_lanes(rows)
    sums = jnp.broadcast_to(total[cols // hd * rows : cols // hd * rows + 1], (rows, LANES))
    ss = jnp.sum(jnp.where(own, sums, 0.0), axis=1, keepdims=True)
    rs = lax.rsqrt(ss / width + EPS)
    keys = k_ref[0]
    row = lax.broadcasted_iota(jnp.int32, (rows, keys.shape[0]), 0)
    scale = jnp.where(row < ints[2], alpha_ref[0], 0.0)
    parts = []
    for h in range(cols // hd):
        q = total[h * rows : (h + 1) * rows] * rs
        r = lax.rsqrt(jnp.mean(q * q, axis=1, keepdims=True) + EPS)
        qn = q * r * gain_ref[...] * (1.0 / math.sqrt(hd))
        qn_ref[:, h * hd : (h + 1) * hd] = qn
        sc = dot32(qn, keys, ROWS_ROWS)
        e = jnp.exp(sc - jnp.max(sc, axis=1, keepdims=True))
        parts.append(scale * e / jnp.sum(e, axis=1, keepdims=True))
    p_ref[...] = jnp.concatenate(parts, axis=1).astype(jnp.bfloat16)


def attend(ints, alpha, width, gain, keys, parts):
    hd = gain.shape[1]
    toks = keys.shape[1]
    heads = 4
    rows = (parts.shape[1] - EXTRA) // heads
    return pl.pallas_call(
        functools.partial(attend_kernel, width),
        grid_spec=pltpu.PrefetchScalarGridSpec(
            num_scalar_prefetch=1,
            grid=(1,),
            in_specs=[
                pl.BlockSpec(memory_space=pltpu.SMEM),
                whole(gain.shape),
                pl.BlockSpec((1,) + keys.shape[1:], lambda k, i: (i[1], 0, 0)),
                whole(parts.shape),
            ],
            out_specs=[whole((rows, heads * toks)), whole((rows, heads * hd))],
        ),
        out_shape=[
            jax.ShapeDtypeStruct((rows, heads * toks), jnp.bfloat16),
            jax.ShapeDtypeStruct((rows, heads * hd), jnp.float32),
        ],
    )(ints, alpha, gain, keys, parts)


def value_out_kernel(slots, v_ref, *refs):
    w_refs, o_ref = refs[:4], refs[4]
    n, vrows, hd = v_ref.shape
    toks = vrows // slots
    heads, chunk = w_refs[0].shape[1] // hd, w_refs[0].shape[2]

    def block(k, carry):
        v = v_ref[k]
        for h in range(heads):
            at = pl.multiple_of((k * heads + h) * toks, toks)
            for j in range(4):
                r = dot16(v, w_refs[j][k, h * hd : (h + 1) * hd, :]).astype(jnp.bfloat16)
                for o in range(slots):
                    o_ref[o, pl.ds(at, toks), j * chunk : (j + 1) * chunk] = r[
                        o * toks : (o + 1) * toks
                    ]
        return carry

    lax.fori_loop(0, n, block, 0)


def value_out(v, w, slots):
    n, vrows, hd = v.shape
    heads = w[0].shape[1] // hd
    chunk = w[0].shape[2]
    toks = vrows // slots
    return pl.pallas_call(
        functools.partial(value_out_kernel, slots),
        in_specs=[pl.BlockSpec(memory_space=pltpu.VMEM)] * 5,
        out_specs=pl.BlockSpec(memory_space=pltpu.VMEM),
        out_shape=jax.ShapeDtypeStruct((slots, n * heads * toks, 4 * chunk), jnp.bfloat16),
        compiler_params=pltpu.CompilerParams(vmem_limit_bytes=VMEM_BYTES),
    )(v, *w)


def back_kernel(qn_ref, k_ref, v_ref, raw_ref, da_ref, gain_ref, o_ref):
    keys, vals, raw, gain = k_ref[0], v_ref[0], raw_ref[0], gain_ref[...]
    hd = keys.shape[1]
    d_kn = jnp.zeros(keys.shape, jnp.float32)
    d_v = jnp.zeros(keys.shape, jnp.float32)
    for h in range(qn_ref.shape[2] // hd):
        qn = qn_ref[0, :, h * hd : (h + 1) * hd]
        da = da_ref[0, :, h * hd : (h + 1) * hd]
        sc = dot32(qn, keys, ROWS_ROWS)
        e = jnp.exp(sc - jnp.max(sc, axis=1, keepdims=True))
        p = e / jnp.sum(e, axis=1, keepdims=True)
        dp = dot32(da, vals, ROWS_ROWS)
        ds = p * (dp - jnp.sum(p * dp, axis=1, keepdims=True))
        d_kn += dot32(ds, qn, COLS_COLS)
        d_v += dot32(p, da, COLS_COLS)
    r = lax.rsqrt(jnp.mean(raw * raw, axis=1, keepdims=True) + EPS)
    u = d_kn * gain
    d_k = r * u - raw * (r * r * r * jnp.mean(raw * u, axis=1, keepdims=True))
    o_ref[0, :, :hd] = d_k.astype(jnp.bfloat16)
    o_ref[0, :, hd:] = d_v.astype(jnp.bfloat16)


def back(qn, keys, vals, raw, da, gain):
    slots, toks, hd = keys.shape
    one = lambda a: pl.BlockSpec((1,) + a.shape[1:], lambda o: (o, 0, 0))
    return pl.pallas_call(
        back_kernel,
        grid=(slots,),
        in_specs=[one(qn), one(keys), one(vals), one(raw), one(da), pl.BlockSpec(gain.shape, lambda o: (0, 0))],
        out_specs=pl.BlockSpec((1, toks, 2 * hd), lambda o: (o, 0, 0)),
        out_shape=jax.ShapeDtypeStruct((slots, toks, 2 * hd), jnp.bfloat16),
    )(qn, keys, vals, raw, da, gain)


def pick(a, i, axis=0):
    return lax.dynamic_index_in_dim(a, i, axis, keepdims=False)


def after(x, *others):
    return lax.optimization_barrier((x,) + others)[0]


def swap(x, axis):
    return lax.all_to_all(x, axis, 0, 0, tiled=True)


def share(x, axis):
    return swap(jnp.broadcast_to(x[None], (lax.axis_size(axis),) + x.shape), axis)


def per_device(
    text, order, lengths, image, in_gain, wq, wk, wv, wo, query_norm_gain, k_gain, gate, cot
):
    D, S, T = lax.axis_size("dp"), lax.axis_size("section"), lax.axis_size("tensor")
    R = T // D
    d, s, t = lax.axis_index("dp"), lax.axis_index("section"), lax.axis_index("tensor")
    slots, rows = text.shape[:2]
    width = in_gain.shape[1]
    hd = k_gain.shape[1]
    feats = width // T
    chunk = feats // D
    toks = image.shape[1] * S

    def onward(x):
        return lax.ppermute(x, "section", [(i, (i + 1) % S) for i in range(S)])

    def dp_flip(x, m):
        return lax.ppermute(x, "dp", [(i, i ^ m) for i in range(D)])

    def dp_all(x):
        across = dp_flip(x, 2)
        return [x, dp_flip(x, 1), across, dp_flip(across, 1)]

    def spread(x):
        parts = jnp.stack(jnp.split(x, D, axis=-1))
        got = swap(jnp.concatenate([parts] * R), "tensor")
        got = pick(got.reshape((D, R) + got.shape[1:]), t // D, 1)
        return jnp.concatenate([pick(got, d ^ j) for j in range(D)], axis=-1)

    def unspread(x, back_sections):
        a, c = t // R, t % D
        parts = jnp.stack(jnp.split(x, D, axis=-1))
        got = []
        for k in range(D):
            pairs = [
                (e * T + b * D + (i + k) % D, (e - back_sections) % S * T + i * R + b)
                for e in range(S)
                for i in range(D)
                for b in range(R)
            ]
            got.append(lax.ppermute(pick(parts, ((c - k) % D) ^ d), ("section", "tensor"), pairs))
        got = jnp.stack(got)
        return jnp.concatenate([pick(got, (j - a) % D) for j in range(D)], axis=-1)

    micro = order[0]
    lens = jnp.take(lengths[0], micro)
    alpha = jnp.tanh(gate)

    wkv = jnp.concatenate([wk[0], wv[0]], axis=1)
    wkv = lax.all_gather(wkv, "dp", axis=0, tiled=True)
    img = jnp.moveaxis(share(jnp.take(image, micro, axis=0), "section"), 0, 1)
    img = after(img.reshape(slots * toks, feats), wkv)
    img = lax.all_gather(img, "tensor", axis=1, tiled=True)
    kv = jnp.dot(img, wkv, preferred_element_type=jnp.float32).reshape(slots, toks, 2 * hd)
    k_raw, vals = kv[..., :hd], kv[..., hd:]
    keys = k_raw * lax.rsqrt(jnp.mean(k_raw * k_raw, axis=-1, keepdims=True) + EPS) * k_gain[0]

    wo_next = onward(wo[0])
    text_f = spread(jnp.take(text, micro, axis=0))
    gain_f = pick(in_gain.reshape(D, T, chunk), t, 1)
    gain_f = jnp.concatenate([pick(gain_f, d ^ j) for j in range(D)])[None]
    wq_own = swap(after(wq[0].reshape(T, chunk, wq.shape[2]), text_f), "tensor")
    wq_f = dp_all(wq_own)
    wo_own = jnp.moveaxis(wo_next.reshape(wo.shape[1], T, chunk), 1, 0)
    wo_own = swap(after(wo_own, wq_own), "tensor")

    probs = h = vo = None
    all_qn, all_h = [], []
    for step in range(S + slots):
        slot_in = jnp.clip(step - s, 0, slots - 1)
        slot_out = jnp.clip(jnp.where(s == 0, step - S, step - s), 0, slots - 1)
        ints = jnp.stack([slot_out, slot_in, lens[slot_in], (s == 0).astype(jnp.int32)])
        last = step == S + slots - 1
        got = front(ints, text_f, gain_f, probs, vo, h, wq_f, last)
        if step > 0:
            all_h.append(got[-1])
        if last:
            break
        parts, hq = got[:2]
        if step == 0:
            wo_f = dp_all(after(wo_own, hq))
        h = onward(hq)
        p, qn = attend(ints, alpha, width, query_norm_gain, keys, swap(parts, "tensor"))
        all_qn.append(qn)
        if step == 0:
            vals16 = vals.astype(jnp.bfloat16).reshape(slots * toks, hd)
            both = share(onward(jnp.concatenate([p, vals16])), "tensor")
            probs = both[:, :rows]
            vo = value_out(both[:, rows:], wo_f, slots)
        else:
            probs = share(onward(p), "tensor")
        if step == 1:
            wo_full = lax.all_gather(after(wo[0], p), "dp", axis=1, tiled=True)
        if step == 5:
            mask = (jnp.arange(rows)[None, :] < lens[:, None]).astype(jnp.float32)[:, :, None]
            d_attn = dot16(cot[0].reshape(slots * rows, width), wo_full, ROWS_ROWS)
            d_attn = alpha[0] * mask * d_attn.reshape(slots, rows, -1)
            probs, d_attn = lax.optimization_barrier((probs, d_attn))

    states = lax.dynamic_slice_in_dim(jnp.stack(all_h), (s - 1) % S, slots, 0)
    states = unspread(states, 1)

    qn = lax.dynamic_slice_in_dim(jnp.stack(all_qn), s, slots, 0)
    d_kv = back(qn, keys, vals, k_raw, d_attn, k_gain).reshape(slots * toks, 2 * hd)
    grad = dot16(d_kv, wkv, ROWS_ROWS).astype(jnp.bfloat16)
    grad = swap(jnp.moveaxis(grad.reshape(slots * toks, T, feats), 1, 0), "tensor")
    grad = jnp.sum(grad.astype(jnp.float32), axis=0).astype(jnp.bfloat16)
    grad = swap(jnp.moveaxis(grad.reshape(slots, S, toks // S, feats), 1, 0), "section")
    grad = jnp.sum(grad.astype(jnp.float32), axis=0)
    grad = jnp.stack([pick(grad, jnp.argmax(micro == m)) for m in range(slots)])
    return (states[None], grad)


def solution(mesh):
    return jax.shard_map(
        per_device,
        mesh=mesh,
        in_specs=(
            P("dp", None, "tensor"),
            P("dp", None),
            P("dp", None),
            P("dp", "section", "tensor"),
            P("section", None),
            P("section", "dp", "tensor"),
            P("section", "dp", "tensor"),
            P("section", "dp", "tensor"),
            P("section", "tensor", "dp"),
            P("section", None),
            P("section", None),
            P("section"),
            P("section", "dp", None, None),
        ),
        out_specs=(P("section", "dp", None, "tensor"), P("dp", "section", "tensor")),
        check_vma=False,
    )
```

```python
import functools
import math

import jax
import jax.numpy as jnp
from jax import lax
from jax.experimental import pallas as pl
from jax.experimental.pallas import tpu as pltpu
from jax.sharding import PartitionSpec as P

EPS = 1e-05
HIGH = lax.Precision.HIGHEST
LANES = 128
EXTRA = 16
VMEM_BYTES = 24 * 2**20
ROWS_ROWS = (((1,), (1,)), ((), ()))
COLS_COLS = (((0,), (0,)), ((), ()))


def dot32(a, b, dims=(((1,), (0,)), ((), ()))):
    return lax.dot_general(a, b, dims, precision=HIGH, preferred_element_type=jnp.float32)


def dot16(a, b, dims=(((1,), (0,)), ((), ()))):
    return lax.dot_general(a, b, dims, preferred_element_type=jnp.float32)


def query_kernel(ints, text_ref, gain_ref, *refs):
    h_ref = refs[0] if len(refs) == 7 else None
    w_refs, q_ref, hq_ref = refs[-6:-2], refs[-2], refs[-1]
    h = text_ref[ints[0]]
    if h_ref is not None:
        h = jnp.where(ints[2] > 0, h, h_ref[...])
    hq_ref[...] = h
    hf = h.astype(jnp.float32)
    x = (hf * gain_ref[...]).astype(jnp.bfloat16)
    ss = jnp.sum(hf * hf, axis=1, keepdims=True)
    hi = ss.astype(jnp.bfloat16).astype(jnp.float32)
    rows = h.shape[0]
    own, lane = own_lanes(rows)
    pair = jnp.where(own, jnp.where(lane < rows, hi, ss - hi), 0.0)
    pair = jnp.broadcast_to(jnp.sum(pair, axis=0, keepdims=True), (EXTRA, LANES))
    pair = pair.astype(jnp.bfloat16)
    n, chunk, cols = w_refs[0].shape
    for k in range(n):
        acc = dot16(x[:, :chunk], w_refs[0][k])
        for j in range(1, 4):
            acc += dot16(x[:, j * chunk : (j + 1) * chunk], w_refs[j][k])
        acc = acc.astype(jnp.bfloat16)
        for i in range(cols // LANES):
            q_ref[k, i * rows : (i + 1) * rows, :] = acc[:, i * LANES : (i + 1) * LANES]
        q_ref[k, cols // LANES * rows :, :] = pair


def query(ints, text, gain, h, w):
    rows, feats = text.shape[1:]
    n, _, cols = w[0].shape
    args = [text, gain] + ([] if h is None else [h]) + list(w)
    return pl.pallas_call(
        query_kernel,
        in_specs=[pl.BlockSpec(memory_space=pltpu.SMEM)]
        + [pl.BlockSpec(memory_space=pltpu.VMEM)] * len(args),
        out_specs=[pl.BlockSpec(memory_space=pltpu.VMEM)] * 2,
        out_shape=[
            jax.ShapeDtypeStruct((n, cols // LANES * rows + EXTRA, LANES), jnp.bfloat16),
            jax.ShapeDtypeStruct((rows, feats), jnp.bfloat16),
        ],
        compiler_params=pltpu.CompilerParams(vmem_limit_bytes=VMEM_BYTES),
    )(ints, *args)


def output_kernel(ints, p_ref, vo_ref, h_ref, o_ref):
    probs = jnp.concatenate([p_ref[i] for i in range(p_ref.shape[0])], axis=1)
    new = h_ref[...].astype(jnp.float32) + dot16(probs, vo_ref[ints[0]])
    o_ref[...] = new.astype(jnp.bfloat16)


def output(ints, probs, vo, h):
    return pl.pallas_call(
        output_kernel,
        in_specs=[pl.BlockSpec(memory_space=pltpu.SMEM)]
        + [pl.BlockSpec(memory_space=pltpu.VMEM)] * 3,
        out_specs=pl.BlockSpec(memory_space=pltpu.VMEM),
        out_shape=jax.ShapeDtypeStruct(h.shape, jnp.bfloat16),
        compiler_params=pltpu.CompilerParams(vmem_limit_bytes=VMEM_BYTES),
    )(ints, probs, vo, h)


def own_lanes(rows):
    row = lax.broadcasted_iota(jnp.int32, (rows, LANES), 0)
    lane = lax.broadcasted_iota(jnp.int32, (rows, LANES), 1)
    return (lane == row) | (lane == row + rows), lane


def whole(shape):
    return pl.BlockSpec(shape, lambda *_: (0,) * len(shape))


def attend_kernel(width, ints, alpha_ref, gain_ref, k_ref, q_ref, p_ref, qn_ref):
    total = q_ref[0].astype(jnp.float32)
    for i in range(1, q_ref.shape[0]):
        total += q_ref[i].astype(jnp.float32)
    hd = gain_ref.shape[1]
    rows, cols = qn_ref.shape
    own, _ = own_lanes(rows)
    sums = jnp.broadcast_to(total[cols // hd * rows : cols // hd * rows + 1], (rows, LANES))
    ss = jnp.sum(jnp.where(own, sums, 0.0), axis=1, keepdims=True)
    rs = lax.rsqrt(ss / width + EPS)
    keys = k_ref[0]
    row = lax.broadcasted_iota(jnp.int32, (rows, keys.shape[0]), 0)
    scale = jnp.where(row < ints[1], alpha_ref[0], 0.0)
    parts = []
    for h in range(cols // hd):
        q = total[h * rows : (h + 1) * rows] * rs
        r = lax.rsqrt(jnp.mean(q * q, axis=1, keepdims=True) + EPS)
        qn = q * r * gain_ref[...] * (1.0 / math.sqrt(hd))
        qn_ref[:, h * hd : (h + 1) * hd] = qn
        sc = dot32(qn, keys, ROWS_ROWS)
        e = jnp.exp(sc - jnp.max(sc, axis=1, keepdims=True))
        parts.append(scale * e / jnp.sum(e, axis=1, keepdims=True))
    p = jnp.concatenate(parts, axis=1).astype(jnp.bfloat16)
    for i in range(p_ref.shape[0]):
        p_ref[i] = p


def attend(ints, alpha, width, gain, keys, parts):
    hd = gain.shape[1]
    toks = keys.shape[1]
    heads = 4
    n = parts.shape[0]
    rows = (parts.shape[1] - EXTRA) // heads
    return pl.pallas_call(
        functools.partial(attend_kernel, width),
        grid_spec=pltpu.PrefetchScalarGridSpec(
            num_scalar_prefetch=1,
            grid=(1,),
            in_specs=[
                pl.BlockSpec(memory_space=pltpu.SMEM),
                whole(gain.shape),
                pl.BlockSpec((1,) + keys.shape[1:], lambda k, i: (i[0], 0, 0)),
                whole(parts.shape),
            ],
            out_specs=[whole((n, rows, heads * toks)), whole((rows, heads * hd))],
        ),
        out_shape=[
            jax.ShapeDtypeStruct((n, rows, heads * toks), jnp.bfloat16),
            jax.ShapeDtypeStruct((rows, heads * hd), jnp.float32),
        ],
    )(ints, alpha, gain, keys, parts)


def value_out_kernel(slots, v_ref, *refs):
    w_refs, o_ref = refs[:4], refs[4]
    n, vrows, hd = v_ref.shape
    toks = vrows // slots
    heads, chunk = w_refs[0].shape[1] // hd, w_refs[0].shape[2]

    def block(k, carry):
        v = v_ref[k]
        for h in range(heads):
            at = pl.multiple_of((k * heads + h) * toks, toks)
            for j in range(4):
                r = dot16(v, w_refs[j][k, h * hd : (h + 1) * hd, :]).astype(jnp.bfloat16)
                for o in range(slots):
                    o_ref[o, pl.ds(at, toks), j * chunk : (j + 1) * chunk] = r[
                        o * toks : (o + 1) * toks
                    ]
        return carry

    lax.fori_loop(0, n, block, 0)


def value_out(v, w, slots):
    n, vrows, hd = v.shape
    heads = w[0].shape[1] // hd
    chunk = w[0].shape[2]
    toks = vrows // slots
    return pl.pallas_call(
        functools.partial(value_out_kernel, slots),
        in_specs=[pl.BlockSpec(memory_space=pltpu.VMEM)] * 5,
        out_specs=pl.BlockSpec(memory_space=pltpu.VMEM),
        out_shape=jax.ShapeDtypeStruct((slots, n * heads * toks, 4 * chunk), jnp.bfloat16),
        compiler_params=pltpu.CompilerParams(vmem_limit_bytes=VMEM_BYTES),
    )(v, *w)


def back_kernel(qn_ref, k_ref, v_ref, raw_ref, da_ref, gain_ref, o_ref):
    keys, vals, raw, gain = k_ref[0], v_ref[0], raw_ref[0], gain_ref[...]
    hd = keys.shape[1]
    d_kn = jnp.zeros(keys.shape, jnp.float32)
    d_v = jnp.zeros(keys.shape, jnp.float32)
    for h in range(qn_ref.shape[2] // hd):
        qn = qn_ref[0, :, h * hd : (h + 1) * hd]
        da = da_ref[0, :, h * hd : (h + 1) * hd]
        sc = dot32(qn, keys, ROWS_ROWS)
        e = jnp.exp(sc - jnp.max(sc, axis=1, keepdims=True))
        p = e / jnp.sum(e, axis=1, keepdims=True)
        dp = dot32(da, vals, ROWS_ROWS)
        ds = p * (dp - jnp.sum(p * dp, axis=1, keepdims=True))
        d_kn += dot32(ds, qn, COLS_COLS)
        d_v += dot32(p, da, COLS_COLS)
    r = lax.rsqrt(jnp.mean(raw * raw, axis=1, keepdims=True) + EPS)
    u = d_kn * gain
    d_k = r * u - raw * (r * r * r * jnp.mean(raw * u, axis=1, keepdims=True))
    o_ref[0, :, :hd] = d_k.astype(jnp.bfloat16)
    o_ref[0, :, hd:] = d_v.astype(jnp.bfloat16)


def back(qn, keys, vals, raw, da, gain):
    slots, toks, hd = keys.shape
    one = lambda a: pl.BlockSpec((1,) + a.shape[1:], lambda o: (o, 0, 0))
    return pl.pallas_call(
        back_kernel,
        grid=(slots,),
        in_specs=[one(qn), one(keys), one(vals), one(raw), one(da), pl.BlockSpec(gain.shape, lambda o: (0, 0))],
        out_specs=pl.BlockSpec((1, toks, 2 * hd), lambda o: (o, 0, 0)),
        out_shape=jax.ShapeDtypeStruct((slots, toks, 2 * hd), jnp.bfloat16),
    )(qn, keys, vals, raw, da, gain)


def pick(a, i, axis=0):
    return lax.dynamic_index_in_dim(a, i, axis, keepdims=False)


def after(x, *others):
    return lax.optimization_barrier((x,) + others)[0]


def swap(x, axis):
    return lax.all_to_all(x, axis, 0, 0, tiled=True)


def share(x, axis):
    return swap(jnp.broadcast_to(x[None], (lax.axis_size(axis),) + x.shape), axis)


def per_device(
    text, order, lengths, image, in_gain, wq, wk, wv, wo, query_norm_gain, k_gain, gate, cot
):
    D, S, T = lax.axis_size("dp"), lax.axis_size("section"), lax.axis_size("tensor")
    R = T // D
    d, s, t = lax.axis_index("dp"), lax.axis_index("section"), lax.axis_index("tensor")
    slots, rows = text.shape[:2]
    width = in_gain.shape[1]
    hd = k_gain.shape[1]
    feats = width // T
    chunk = feats // D
    toks = image.shape[1] * S

    def onward(x):
        return lax.ppermute(x, "section", [(i, (i + 1) % S) for i in range(S)])

    def dp_flip(x, m):
        return lax.ppermute(x, "dp", [(i, i ^ m) for i in range(D)])

    def dp_all(x):
        across = dp_flip(x, 2)
        return [x, dp_flip(x, 1), across, dp_flip(across, 1)]

    def spread(x):
        parts = jnp.stack(jnp.split(x, D, axis=-1))
        got = swap(jnp.concatenate([parts] * R), "tensor")
        got = pick(got.reshape((D, R) + got.shape[1:]), t // D, 1)
        return jnp.concatenate([pick(got, d ^ j) for j in range(D)], axis=-1)

    def unspread(x):
        a, c = t // R, t % D
        parts = jnp.stack(jnp.split(x, D, axis=-1))
        got = []
        for k in range(D):
            pairs = [(b * D + (i + k) % D, i * R + b) for i in range(D) for b in range(R)]
            got.append(lax.ppermute(pick(parts, ((c - k) % D) ^ d), "tensor", pairs))
        got = jnp.stack(got)
        return jnp.concatenate([pick(got, (j - a) % D) for j in range(D)], axis=-1)

    micro = order[0]
    lens = jnp.take(lengths[0], micro)
    alpha = jnp.tanh(gate)

    wkv = jnp.concatenate([wk[0], wv[0]], axis=1)
    wkv = lax.all_gather(wkv, "dp", axis=0, tiled=True)
    shared = share(jnp.take(image, micro, axis=0), "section")
    img = jnp.moveaxis(shared, 0, 1)
    img = after(img.reshape(slots * toks, feats), wkv)
    img = lax.all_gather(img, "tensor", axis=1, tiled=True)
    kv = jnp.dot(img, wkv, preferred_element_type=jnp.float32).reshape(slots, toks, 2 * hd)
    k_raw, vals = kv[..., :hd], kv[..., hd:]
    keys = k_raw * lax.rsqrt(jnp.mean(k_raw * k_raw, axis=-1, keepdims=True) + EPS) * k_gain[0]

    text_f = spread(after(jnp.take(text, micro, axis=0), shared))
    gain_f = pick(in_gain.reshape(D, T, chunk), t, 1)
    gain_f = jnp.concatenate([pick(gain_f, d ^ j) for j in range(D)])[None]
    wq_own = swap(after(wq[0].reshape(T, chunk, wq.shape[2]), text_f), "tensor")
    wq_f = dp_all(wq_own)
    wo_own = jnp.moveaxis(wo[0].reshape(wo.shape[1], T, chunk), 1, 0)
    wo_own = swap(after(wo_own, wq_own), "tensor")

    h = None
    all_qn, all_h = [], []
    for step in range(S + slots - 1):
        slot = jnp.clip(step - s, 0, slots - 1)
        ints = jnp.stack([slot, lens[slot], (s == 0).astype(jnp.int32)])
        parts, hq = query(ints, text_f, gain_f, h, wq_f)
        if step == 0:
            wo_f = dp_all(after(wo_own, hq))
        p, qn = attend(ints, alpha, width, query_norm_gain, keys, swap(parts, "tensor"))
        all_qn.append(qn)
        if step == 0:
            vals16 = vals.astype(jnp.bfloat16).reshape(slots * toks, hd)
            vals16 = jnp.broadcast_to(vals16[None], (T,) + vals16.shape)
            both = swap(jnp.concatenate([p, vals16], axis=1), "tensor")
            probs = both[:, :rows]
            vo = value_out(both[:, rows:], wo_f, slots)
        else:
            probs = swap(p, "tensor")
        if step == 1:
            wo_full = lax.all_gather(after(wo[0], p), "dp", axis=1, tiled=True)
        if step == 5:
            mask = (jnp.arange(rows)[None, :] < lens[:, None]).astype(jnp.float32)[:, :, None]
            d_attn = dot16(cot[0].reshape(slots * rows, width), wo_full, ROWS_ROWS)
            d_attn = alpha[0] * mask * d_attn.reshape(slots, rows, -1)
            probs, d_attn = lax.optimization_barrier((probs, d_attn))
        h = output(ints, probs, vo, hq)
        all_h.append(h)
        h = onward(h)

    states = unspread(lax.dynamic_slice_in_dim(jnp.stack(all_h), s, slots, 0))

    qn = lax.dynamic_slice_in_dim(jnp.stack(all_qn), s, slots, 0)
    d_kv = back(qn, keys, vals, k_raw, d_attn, k_gain).reshape(slots * toks, 2 * hd)
    grad = dot16(d_kv, wkv, ROWS_ROWS).astype(jnp.bfloat16)
    grad = swap(jnp.moveaxis(grad.reshape(slots * toks, T, feats), 1, 0), "tensor")
    grad = jnp.sum(grad.astype(jnp.float32), axis=0).astype(jnp.bfloat16)
    grad = swap(jnp.moveaxis(grad.reshape(slots, S, toks // S, feats), 1, 0), "section")
    grad = jnp.sum(grad.astype(jnp.float32), axis=0)
    grad = jnp.stack([pick(grad, jnp.argmax(micro == m)) for m in range(slots)])
    return (states[None], grad)


def solution(mesh):
    return jax.shard_map(
        per_device,
        mesh=mesh,
        in_specs=(
            P("dp", None, "tensor"),
            P("dp", None),
            P("dp", None),
            P("dp", "section", "tensor"),
            P("section", None),
            P("section", "dp", "tensor"),
            P("section", "dp", "tensor"),
            P("section", "dp", "tensor"),
            P("section", "tensor", "dp"),
            P("section", None),
            P("section", None),
            P("section"),
            P("section", "dp", None, None),
        ),
        out_specs=(P("section", "dp", None, "tensor"), P("dp", "section", "tensor")),
        check_vma=False,
    )
```

```python
import functools
import math

import jax
import jax.numpy as jnp
from jax import lax
from jax.experimental import pallas as pl
from jax.experimental.pallas import tpu as pltpu
from jax.sharding import PartitionSpec as P

EPS = 1e-05
HIGH = lax.Precision.HIGHEST
LANES = 128
EXTRA = 16
VMEM_BYTES = 14 * 2**20
ROWS_ROWS = (((1,), (1,)), ((), ()))
COLS_COLS = (((0,), (0,)), ((), ()))


def dot32(a, b, dims=(((1,), (0,)), ((), ()))):
    return lax.dot_general(a, b, dims, precision=HIGH, preferred_element_type=jnp.float32)


def dot16(a, b, dims=(((1,), (0,)), ((), ()))):
    return lax.dot_general(a, b, dims, preferred_element_type=jnp.float32)


def slot_of(step, ints, slots):
    return jnp.clip(step - ints[0], 0, slots - 1)


def query_kernel(step, ints, text_ref, gain_ref, *refs):
    h_ref = refs[0] if len(refs) == 7 else None
    w_refs, q_ref, hq_ref = refs[-6:-2], refs[-2], refs[-1]
    h = text_ref[slot_of(step, ints, text_ref.shape[0])]
    if h_ref is not None:
        h = jnp.where(ints[0] == 0, h, h_ref[...])
    hq_ref[...] = h
    hf = h.astype(jnp.float32)
    x = (hf * gain_ref[...]).astype(jnp.bfloat16)
    ss = jnp.sum(hf * hf, axis=1, keepdims=True)
    hi = ss.astype(jnp.bfloat16).astype(jnp.float32)
    rows = h.shape[0]
    own, lane = own_lanes(rows)
    pair = jnp.where(own, jnp.where(lane < rows, hi, ss - hi), 0.0)
    pair = jnp.broadcast_to(jnp.sum(pair, axis=0, keepdims=True), (EXTRA, LANES))
    pair = pair.astype(jnp.bfloat16)
    n, chunk, cols = w_refs[0].shape
    for k in range(n):
        acc = dot16(x[:, :chunk], w_refs[0][k])
        for j in range(1, 4):
            acc += dot16(x[:, j * chunk : (j + 1) * chunk], w_refs[j][k])
        acc = acc.astype(jnp.bfloat16)
        for i in range(cols // LANES):
            q_ref[k, i * rows : (i + 1) * rows, :] = acc[:, i * LANES : (i + 1) * LANES]
        q_ref[k, cols // LANES * rows :, :] = pair


def query(step, ints, text, gain, h, w):
    rows, feats = text.shape[1:]
    n, _, cols = w[0].shape
    args = [text, gain] + ([] if h is None else [h]) + list(w)
    return pl.pallas_call(
        functools.partial(query_kernel, step),
        in_specs=[pl.BlockSpec(memory_space=pltpu.SMEM)]
        + [pl.BlockSpec(memory_space=pltpu.VMEM)] * len(args),
        out_specs=[pl.BlockSpec(memory_space=pltpu.VMEM)] * 2,
        out_shape=[
            jax.ShapeDtypeStruct((n, cols // LANES * rows + EXTRA, LANES), jnp.bfloat16),
            jax.ShapeDtypeStruct((rows, feats), jnp.bfloat16),
        ],
        compiler_params=pltpu.CompilerParams(vmem_limit_bytes=VMEM_BYTES),
    )(ints, *args)


def output_kernel(step, ints, p_ref, vo_ref, h_ref, o_ref):
    probs = jnp.concatenate([p_ref[i] for i in range(p_ref.shape[0])], axis=1)
    new = h_ref[...].astype(jnp.float32) + dot16(probs, vo_ref[slot_of(step, ints, vo_ref.shape[0])])
    o_ref[...] = new.astype(jnp.bfloat16)


def output(step, ints, probs, vo, h):
    return pl.pallas_call(
        functools.partial(output_kernel, step),
        in_specs=[pl.BlockSpec(memory_space=pltpu.SMEM)]
        + [pl.BlockSpec(memory_space=pltpu.VMEM)] * 3,
        out_specs=pl.BlockSpec(memory_space=pltpu.VMEM),
        out_shape=jax.ShapeDtypeStruct(h.shape, jnp.bfloat16),
        compiler_params=pltpu.CompilerParams(vmem_limit_bytes=VMEM_BYTES),
    )(ints, probs, vo, h)


def own_lanes(rows):
    row = lax.broadcasted_iota(jnp.int32, (rows, LANES), 0)
    lane = lax.broadcasted_iota(jnp.int32, (rows, LANES), 1)
    return (lane == row) | (lane == row + rows), lane


def whole(shape):
    return pl.BlockSpec(shape, lambda *_: (0,) * len(shape))


def attend_kernel(step, width, ints, alpha_ref, gain_ref, k_ref, q_ref, p_ref, qn_ref):
    slot = slot_of(step, ints, k_ref.shape[0])
    total = q_ref[0].astype(jnp.float32)
    for i in range(1, q_ref.shape[0]):
        total += q_ref[i].astype(jnp.float32)
    hd = gain_ref.shape[1]
    rows, cols = qn_ref.shape
    own, _ = own_lanes(rows)
    sums = jnp.broadcast_to(total[cols // hd * rows : cols // hd * rows + 1], (rows, LANES))
    ss = jnp.sum(jnp.where(own, sums, 0.0), axis=1, keepdims=True)
    rs = lax.rsqrt(ss / width + EPS)
    keys = k_ref[slot]
    row = lax.broadcasted_iota(jnp.int32, (rows, keys.shape[0]), 0)
    scale = jnp.where(row < ints[1 + slot], alpha_ref[0], 0.0)
    parts = []
    for h in range(cols // hd):
        q = total[h * rows : (h + 1) * rows] * rs
        r = lax.rsqrt(jnp.mean(q * q, axis=1, keepdims=True) + EPS)
        qn = q * r * gain_ref[...] * (1.0 / math.sqrt(hd))
        qn_ref[:, h * hd : (h + 1) * hd] = qn
        sc = dot32(qn, keys, ROWS_ROWS)
        e = jnp.exp(sc - jnp.max(sc, axis=1, keepdims=True))
        parts.append(scale * e / jnp.sum(e, axis=1, keepdims=True))
    p = jnp.concatenate(parts, axis=1).astype(jnp.bfloat16)
    for i in range(p_ref.shape[0]):
        p_ref[i] = p


def attend(step, ints, alpha, width, gain, keys, parts):
    hd = gain.shape[1]
    toks = keys.shape[1]
    heads = 4
    n = parts.shape[0]
    rows = (parts.shape[1] - EXTRA) // heads
    return pl.pallas_call(
        functools.partial(attend_kernel, step, width),
        in_specs=[pl.BlockSpec(memory_space=pltpu.SMEM)] * 2
        + [pl.BlockSpec(memory_space=pltpu.VMEM)] * 3,
        out_specs=[pl.BlockSpec(memory_space=pltpu.VMEM)] * 2,
        out_shape=[
            jax.ShapeDtypeStruct((n, rows, heads * toks), jnp.bfloat16),
            jax.ShapeDtypeStruct((rows, heads * hd), jnp.float32),
        ],
        compiler_params=pltpu.CompilerParams(vmem_limit_bytes=VMEM_BYTES),
    )(ints, alpha, gain, keys, parts)


def value_out_kernel(slots, v_ref, *refs):
    w_refs, o_ref = refs[:4], refs[4]
    n, vrows, hd = v_ref.shape
    toks = vrows // slots
    heads, chunk = w_refs[0].shape[1] // hd, w_refs[0].shape[2]

    def block(k, carry):
        v = v_ref[k]
        for h in range(heads):
            at = pl.multiple_of((k * heads + h) * toks, toks)
            for j in range(4):
                r = dot16(v, w_refs[j][k, h * hd : (h + 1) * hd, :]).astype(jnp.bfloat16)
                for o in range(slots):
                    o_ref[o, pl.ds(at, toks), j * chunk : (j + 1) * chunk] = r[
                        o * toks : (o + 1) * toks
                    ]
        return carry

    lax.fori_loop(0, n, block, 0)


def value_out(v, w, slots):
    n, vrows, hd = v.shape
    heads = w[0].shape[1] // hd
    chunk = w[0].shape[2]
    toks = vrows // slots
    return pl.pallas_call(
        functools.partial(value_out_kernel, slots),
        in_specs=[pl.BlockSpec(memory_space=pltpu.VMEM)] * 5,
        out_specs=pl.BlockSpec(memory_space=pltpu.VMEM),
        out_shape=jax.ShapeDtypeStruct((slots, n * heads * toks, 4 * chunk), jnp.bfloat16),
        compiler_params=pltpu.CompilerParams(vmem_limit_bytes=VMEM_BYTES),
    )(v, *w)


def back_kernel(qn_ref, k_ref, v_ref, raw_ref, da_ref, gain_ref, o_ref):
    keys, vals, raw, gain = k_ref[0], v_ref[0], raw_ref[0], gain_ref[...]
    hd = keys.shape[1]
    d_kn = jnp.zeros(keys.shape, jnp.float32)
    d_v = jnp.zeros(keys.shape, jnp.float32)
    for h in range(qn_ref.shape[2] // hd):
        qn = qn_ref[0, :, h * hd : (h + 1) * hd]
        da = da_ref[0, :, h * hd : (h + 1) * hd]
        sc = dot32(qn, keys, ROWS_ROWS)
        e = jnp.exp(sc - jnp.max(sc, axis=1, keepdims=True))
        p = e / jnp.sum(e, axis=1, keepdims=True)
        dp = dot32(da, vals, ROWS_ROWS)
        ds = p * (dp - jnp.sum(p * dp, axis=1, keepdims=True))
        d_kn += dot32(ds, qn, COLS_COLS)
        d_v += dot32(p, da, COLS_COLS)
    r = lax.rsqrt(jnp.mean(raw * raw, axis=1, keepdims=True) + EPS)
    u = d_kn * gain
    d_k = r * u - raw * (r * r * r * jnp.mean(raw * u, axis=1, keepdims=True))
    o_ref[0, :, :hd] = d_k.astype(jnp.bfloat16)
    o_ref[0, :, hd:] = d_v.astype(jnp.bfloat16)


def back(qn, keys, vals, raw, da, gain):
    slots, toks, hd = keys.shape
    one = lambda a: pl.BlockSpec((1,) + a.shape[1:], lambda o: (o, 0, 0))
    return pl.pallas_call(
        back_kernel,
        grid=(slots,),
        in_specs=[one(qn), one(keys), one(vals), one(raw), one(da), pl.BlockSpec(gain.shape, lambda o: (0, 0))],
        out_specs=pl.BlockSpec((1, toks, 2 * hd), lambda o: (o, 0, 0)),
        out_shape=jax.ShapeDtypeStruct((slots, toks, 2 * hd), jnp.bfloat16),
    )(qn, keys, vals, raw, da, gain)


def pick(a, i, axis=0):
    return lax.dynamic_index_in_dim(a, i, axis, keepdims=False)


def after(x, *others):
    return lax.optimization_barrier((x,) + others)[0]


def swap(x, axis):
    return lax.all_to_all(x, axis, 0, 0, tiled=True)


def share(x, axis):
    return swap(jnp.broadcast_to(x[None], (lax.axis_size(axis),) + x.shape), axis)


def per_device(
    text, order, lengths, image, in_gain, wq, wk, wv, wo, query_norm_gain, k_gain, gate, cot
):
    D, S, T = lax.axis_size("dp"), lax.axis_size("section"), lax.axis_size("tensor")
    R = T // D
    d, s, t = lax.axis_index("dp"), lax.axis_index("section"), lax.axis_index("tensor")
    slots, rows = text.shape[:2]
    width = in_gain.shape[1]
    hd = k_gain.shape[1]
    feats = width // T
    chunk = feats // D
    toks = image.shape[1] * S

    def onward(x):
        return lax.ppermute(x, "section", [(i, (i + 1) % S) for i in range(S)])

    def dp_flip(x, m):
        return lax.ppermute(x, "dp", [(i, i ^ m) for i in range(D)])

    def dp_all(x):
        across = dp_flip(x, 2)
        return [x, dp_flip(x, 1), across, dp_flip(across, 1)]

    def spread(x):
        a, c = t // R, t % D
        parts = jnp.stack(jnp.split(x, D, axis=-1))
        got = []
        for k in range(D):
            pairs = [(i * R + b, b * D + (i + k) % D) for i in range(D) for b in range(R)]
            got.append(lax.ppermute(pick(parts, (a + k) % D), "tensor", pairs))
        got = jnp.stack(got)
        return jnp.concatenate([pick(got, (c - (d ^ j)) % D) for j in range(D)], axis=-1)

    def unspread(x):
        a, c = t // R, t % D
        parts = jnp.stack(jnp.split(x, D, axis=-1))
        got = []
        for k in range(D):
            pairs = [(b * D + (i + k) % D, i * R + b) for i in range(D) for b in range(R)]
            got.append(lax.ppermute(pick(parts, ((c - k) % D) ^ d), "tensor", pairs))
        got = jnp.stack(got)
        return jnp.concatenate([pick(got, (j - a) % D) for j in range(D)], axis=-1)

    micro = order[0]
    lens = jnp.take(lengths[0], micro)
    alpha = jnp.tanh(gate)

    shared = share(jnp.take(image, micro, axis=0).reshape(-1, feats), "section")
    img = lax.all_gather(shared.reshape(slots * toks, feats), "tensor", axis=1, tiled=True)
    wkv = after(jnp.concatenate([wk[0], wv[0]], axis=1), img)
    wkv = lax.all_gather(wkv, "dp", axis=0, tiled=True)
    kv = jnp.dot(img, wkv, preferred_element_type=jnp.float32)
    kv = jnp.moveaxis(kv.reshape(S, slots, toks // S, 2 * hd), 0, 1).reshape(slots, toks, 2 * hd)
    k_raw, vals = kv[..., :hd], kv[..., hd:]
    keys = k_raw * lax.rsqrt(jnp.mean(k_raw * k_raw, axis=-1, keepdims=True) + EPS) * k_gain[0]

    wq_own = swap(after(wq[0].reshape(T, chunk, wq.shape[2]), shared), "tensor")
    wq_f = dp_all(wq_own)
    text_f = spread(after(jnp.take(text, micro, axis=0), wq_own))
    gain_f = pick(in_gain.reshape(D, T, chunk), t, 1)
    gain_f = jnp.concatenate([pick(gain_f, d ^ j) for j in range(D)])[None]
    wo_own = jnp.moveaxis(wo[0].reshape(wo.shape[1], T, chunk), 1, 0)
    wo_own = swap(after(wo_own, wq_own, wkv), "tensor")
    ints = jnp.concatenate([s.astype(jnp.int32)[None], lens])

    h = None
    all_qn, all_h = [], []
    for step in range(S + slots - 1):
        parts, hq = query(step, ints, text_f, gain_f, h, wq_f)
        p, qn = attend(step, ints, alpha, width, query_norm_gain, keys, swap(parts, "tensor"))
        all_qn.append(qn)
        if step == 0:
            vals16 = vals.astype(jnp.bfloat16).reshape(slots * toks, hd)
            vals16 = jnp.broadcast_to(vals16[None], (T,) + vals16.shape)
            both = swap(jnp.concatenate([p, vals16], axis=1), "tensor")
            probs = both[:, :rows]
            wo_own = after(wo_own, hq)
            across = dp_flip(wo_own, 2)
            wo_f = [wo_own, dp_flip(wo_own, 1), across, dp_flip(after(across, probs), 1)]
            vo = value_out(both[:, rows:], wo_f, slots)
        else:
            probs = swap(p, "tensor")
        if step == 1:
            wo_full = lax.all_gather(after(wo[0], p), "dp", axis=1, tiled=True)
        if step == 5:
            mask = (jnp.arange(rows)[None, :] < lens[:, None]).astype(jnp.float32)[:, :, None]
            d_attn = dot16(cot[0].reshape(slots * rows, width), wo_full, ROWS_ROWS)
            d_attn = alpha[0] * mask * d_attn.reshape(slots, rows, -1)
            probs, d_attn = lax.optimization_barrier((probs, d_attn))
        h = output(step, ints, probs, vo, hq)
        all_h.append(h)
        h = onward(h)

    states = unspread(lax.dynamic_slice_in_dim(jnp.stack(all_h), s, slots, 0))

    qn = lax.dynamic_slice_in_dim(jnp.stack(all_qn), s, slots, 0)
    d_kv = back(qn, keys, vals, k_raw, d_attn, k_gain).reshape(slots * toks, 2 * hd)
    grad = dot16(d_kv, wkv, ROWS_ROWS).astype(jnp.bfloat16)
    grad = swap(jnp.moveaxis(grad.reshape(slots * toks, T, feats), 1, 0), "tensor")
    grad = jnp.sum(grad.astype(jnp.float32), axis=0).astype(jnp.bfloat16)
    grad = swap(jnp.moveaxis(grad.reshape(slots, S, toks // S, feats), 1, 0), "section")
    grad = jnp.sum(grad.astype(jnp.float32), axis=0)
    grad = jnp.stack([pick(grad, jnp.argmax(micro == m)) for m in range(slots)])
    return (states[None], grad)


def solution(mesh):
    return jax.shard_map(
        per_device,
        mesh=mesh,
        in_specs=(
            P("dp", None, "tensor"),
            P("dp", None),
            P("dp", None),
            P("dp", "section", "tensor"),
            P("section", None),
            P("section", "dp", "tensor"),
            P("section", "dp", "tensor"),
            P("section", "dp", "tensor"),
            P("section", "tensor", "dp"),
            P("section", None),
            P("section", None),
            P("section"),
            P("section", "dp", None, None),
        ),
        out_specs=(P("section", "dp", None, "tensor"), P("dp", "section", "tensor")),
        check_vma=False,
    )
```

```python
import functools
import math

import jax
import jax.numpy as jnp
from jax import lax
from jax.experimental import pallas as pl
from jax.experimental.pallas import tpu as pltpu
from jax.sharding import PartitionSpec as P

EPS = 1e-05
HIGH = lax.Precision.HIGHEST
LANES = 128
EXTRA = 16
VMEM_BYTES = 14 * 2**20
ROWS_ROWS = (((1,), (1,)), ((), ()))
COLS_COLS = (((0,), (0,)), ((), ()))


def dot32(a, b, dims=(((1,), (0,)), ((), ()))):
    return lax.dot_general(a, b, dims, precision=HIGH, preferred_element_type=jnp.float32)


def dot16(a, b, dims=(((1,), (0,)), ((), ()))):
    return lax.dot_general(a, b, dims, preferred_element_type=jnp.float32)


def slot_of(step, ints, slots):
    return jnp.clip(step - ints[0], 0, slots - 1)


def query_kernel(step, ints, text_ref, gain_ref, *refs):
    h_ref = refs[0] if len(refs) == 9 else None
    w_refs, q_ref, hq_ref, w_s, sems = refs[-8:-4], refs[-4], refs[-3], refs[-2], refs[-1]
    n, chunk, cols = w_refs[0].shape
    copies = []
    for half in range(2):
        at = pl.ds(half * (n // 2), n // 2)
        for j in range(4):
            copy = pltpu.make_async_copy(w_refs[j].at[at], w_s.at[j, at], sems.at[half, j])
            copy.start()
            copies.append(copy)
    h = text_ref[slot_of(step, ints, text_ref.shape[0])]
    if h_ref is not None:
        h = jnp.where(ints[0] == 0, h, h_ref[...])
    hq_ref[...] = h
    hf = h.astype(jnp.float32)
    x = (hf * gain_ref[...]).astype(jnp.bfloat16)
    ss = jnp.sum(hf * hf, axis=1, keepdims=True)
    hi = ss.astype(jnp.bfloat16).astype(jnp.float32)
    rows = h.shape[0]
    own, lane = own_lanes(rows)
    pair = jnp.where(own, jnp.where(lane < rows, hi, ss - hi), 0.0)
    pair = jnp.broadcast_to(jnp.sum(pair, axis=0, keepdims=True), (EXTRA, LANES))
    pair = pair.astype(jnp.bfloat16)
    for k in range(n):
        if k % (n // 2) == 0:
            for copy in copies[k // (n // 2) * 4 :][:4]:
                copy.wait()
        acc = dot16(x[:, :chunk], w_s[0, k])
        for j in range(1, 4):
            acc += dot16(x[:, j * chunk : (j + 1) * chunk], w_s[j, k])
        acc = acc.astype(jnp.bfloat16)
        for i in range(cols // LANES):
            q_ref[k, i * rows : (i + 1) * rows, :] = acc[:, i * LANES : (i + 1) * LANES]
        q_ref[k, cols // LANES * rows :, :] = pair


def query(step, ints, text, gain, h, w):
    rows, feats = text.shape[1:]
    n, chunk, cols = w[0].shape
    args = [text, gain] + ([] if h is None else [h])
    return pl.pallas_call(
        functools.partial(query_kernel, step),
        in_specs=[pl.BlockSpec(memory_space=pltpu.SMEM)]
        + [pl.BlockSpec(memory_space=pltpu.VMEM)] * len(args)
        + [pl.BlockSpec(memory_space=pl.ANY)] * 4,
        out_specs=[pl.BlockSpec(memory_space=pltpu.VMEM)] * 2,
        out_shape=[
            jax.ShapeDtypeStruct((n, cols // LANES * rows + EXTRA, LANES), jnp.bfloat16),
            jax.ShapeDtypeStruct((rows, feats), jnp.bfloat16),
        ],
        scratch_shapes=[
            pltpu.VMEM((4, n, chunk, cols), jnp.bfloat16),
            pltpu.SemaphoreType.DMA((2, 4)),
        ],
        compiler_params=pltpu.CompilerParams(vmem_limit_bytes=VMEM_BYTES),
    )(ints, *args, *w)


def keep(step, ints, kept_ref, new, old_ref):
    for o in range(kept_ref.shape[0]):
        old = jnp.zeros(new.shape, new.dtype) if old_ref is None else old_ref[o]
        kept_ref[o] = jnp.where(step - ints[0] == o, new, old)


def output_kernel(step, ints, p_ref, vo_ref, h_ref, *refs):
    o_ref, kept_ref = refs[-2:]
    probs = jnp.concatenate([p_ref[i] for i in range(p_ref.shape[0])], axis=1)
    new = h_ref[...].astype(jnp.float32) + dot16(probs, vo_ref[slot_of(step, ints, vo_ref.shape[0])])
    new = new.astype(jnp.bfloat16)
    o_ref[...] = new
    keep(step, ints, kept_ref, new, refs[0] if len(refs) == 3 else None)


def output(step, ints, probs, vo, h, kept):
    args = [probs, vo, h] + ([] if kept is None else [kept])
    return pl.pallas_call(
        functools.partial(output_kernel, step),
        in_specs=[pl.BlockSpec(memory_space=pltpu.SMEM)]
        + [pl.BlockSpec(memory_space=pltpu.VMEM)] * len(args),
        out_specs=[pl.BlockSpec(memory_space=pltpu.VMEM)] * 2,
        out_shape=[
            jax.ShapeDtypeStruct(h.shape, jnp.bfloat16),
            jax.ShapeDtypeStruct(vo.shape[:1] + h.shape, jnp.bfloat16),
        ],
        compiler_params=pltpu.CompilerParams(vmem_limit_bytes=VMEM_BYTES),
    )(ints, *args)


def own_lanes(rows):
    row = lax.broadcasted_iota(jnp.int32, (rows, LANES), 0)
    lane = lax.broadcasted_iota(jnp.int32, (rows, LANES), 1)
    return (lane == row) | (lane == row + rows), lane


def whole(shape):
    return pl.BlockSpec(shape, lambda *_: (0,) * len(shape))


def attend_kernel(step, width, ints, alpha_ref, gain_ref, k_ref, q_ref, *refs):
    p_ref, kept_ref = refs[-2:]
    slot = slot_of(step, ints, k_ref.shape[0])
    total = q_ref[0].astype(jnp.float32)
    for i in range(1, q_ref.shape[0]):
        total += q_ref[i].astype(jnp.float32)
    hd = gain_ref.shape[1]
    rows, cols = kept_ref.shape[1:]
    own, _ = own_lanes(rows)
    sums = jnp.broadcast_to(total[cols // hd * rows : cols // hd * rows + 1], (rows, LANES))
    ss = jnp.sum(jnp.where(own, sums, 0.0), axis=1, keepdims=True)
    rs = lax.rsqrt(ss / width + EPS)
    keys = k_ref[slot]
    row = lax.broadcasted_iota(jnp.int32, (rows, keys.shape[0]), 0)
    scale = jnp.where(row < ints[1 + slot], alpha_ref[0], 0.0)
    parts, normed = [], []
    for h in range(cols // hd):
        q = total[h * rows : (h + 1) * rows] * rs
        r = lax.rsqrt(jnp.mean(q * q, axis=1, keepdims=True) + EPS)
        qn = q * r * gain_ref[...] * (1.0 / math.sqrt(hd))
        normed.append(qn)
        sc = dot32(qn, keys, ROWS_ROWS)
        e = jnp.exp(sc - jnp.max(sc, axis=1, keepdims=True))
        parts.append(scale * e / jnp.sum(e, axis=1, keepdims=True))
    p = jnp.concatenate(parts, axis=1).astype(jnp.bfloat16)
    for i in range(p_ref.shape[0]):
        p_ref[i] = p
    old_ref = refs[0] if len(refs) == 3 else None
    keep(step, ints, kept_ref, jnp.concatenate(normed, axis=1), old_ref)


def attend(step, ints, alpha, width, gain, keys, parts, kept):
    hd = gain.shape[1]
    toks = keys.shape[1]
    heads = 4
    n = parts.shape[0]
    rows = (parts.shape[1] - EXTRA) // heads
    args = [gain, keys, parts] + ([] if kept is None else [kept])
    return pl.pallas_call(
        functools.partial(attend_kernel, step, width),
        in_specs=[pl.BlockSpec(memory_space=pltpu.SMEM)] * 2
        + [pl.BlockSpec(memory_space=pltpu.VMEM)] * len(args),
        out_specs=[pl.BlockSpec(memory_space=pltpu.VMEM)] * 2,
        out_shape=[
            jax.ShapeDtypeStruct((n, rows, heads * toks), jnp.bfloat16),
            jax.ShapeDtypeStruct(keys.shape[:1] + (rows, heads * hd), jnp.float32),
        ],
        compiler_params=pltpu.CompilerParams(vmem_limit_bytes=VMEM_BYTES),
    )(ints, alpha, *args)


def value_out_kernel(slots, v_ref, *refs):
    w_refs, o_ref = refs[:-1], refs[-1]
    n, vrows, hd = v_ref.shape
    toks = vrows // slots
    part, chunk = w_refs[0].shape[1] // hd, w_refs[0].shape[2]
    heads = part * len(w_refs) // 4

    def block(k, carry):
        v = v_ref[k]
        for h in range(heads):
            at = pl.multiple_of((k * heads + h) * toks, toks)
            for j in range(4):
                w_ref = w_refs[h // part * 4 + j]
                i = h % part * hd
                r = dot16(v, w_ref[k, i : i + hd, :]).astype(jnp.bfloat16)
                for o in range(slots):
                    o_ref[o, pl.ds(at, toks), j * chunk : (j + 1) * chunk] = r[
                        o * toks : (o + 1) * toks
                    ]
        return carry

    lax.fori_loop(0, n, block, 0)


def value_out(v, w, slots):
    n, vrows, hd = v.shape
    heads = w[0].shape[1] * len(w) // 4 // hd
    chunk = w[0].shape[2]
    toks = vrows // slots
    return pl.pallas_call(
        functools.partial(value_out_kernel, slots),
        in_specs=[pl.BlockSpec(memory_space=pltpu.VMEM)] * (1 + len(w)),
        out_specs=pl.BlockSpec(memory_space=pltpu.VMEM),
        out_shape=jax.ShapeDtypeStruct((slots, n * heads * toks, 4 * chunk), jnp.bfloat16),
        compiler_params=pltpu.CompilerParams(vmem_limit_bytes=2 * VMEM_BYTES),
    )(v, *w)


def back_kernel(slot, qn_ref, k_ref, v_ref, raw_ref, da_ref, gain_ref, w_ref, o_ref):
    keys, vals, raw, gain = k_ref[slot], v_ref[slot], raw_ref[slot], gain_ref[...]
    hd = keys.shape[1]
    d_kn = jnp.zeros(keys.shape, jnp.float32)
    d_v = jnp.zeros(keys.shape, jnp.float32)
    for h in range(qn_ref.shape[2] // hd):
        qn = qn_ref[slot, :, h * hd : (h + 1) * hd]
        da = da_ref[slot, :, h * hd : (h + 1) * hd]
        sc = dot32(qn, keys, ROWS_ROWS)
        e = jnp.exp(sc - jnp.max(sc, axis=1, keepdims=True))
        p = e / jnp.sum(e, axis=1, keepdims=True)
        dp = dot32(da, vals, ROWS_ROWS)
        ds = p * (dp - jnp.sum(p * dp, axis=1, keepdims=True))
        d_kn += dot32(ds, qn, COLS_COLS)
        d_v += dot32(p, da, COLS_COLS)
    r = lax.rsqrt(jnp.mean(raw * raw, axis=1, keepdims=True) + EPS)
    u = d_kn * gain
    d_k = r * u - raw * (r * r * r * jnp.mean(raw * u, axis=1, keepdims=True))
    d_kv = jnp.concatenate([d_k, d_v], axis=1).astype(jnp.bfloat16)
    feats = o_ref.shape[2]
    for i in range(o_ref.shape[0]):
        part = dot16(d_kv, w_ref[i * feats : (i + 1) * feats], ROWS_ROWS)
        o_ref[i] = part.astype(jnp.bfloat16)


def back(slot, n, qn, keys, vals, raw, da, gain, w):
    args = (qn, keys, vals, raw, da, gain, w)
    return pl.pallas_call(
        functools.partial(back_kernel, slot),
        in_specs=[pl.BlockSpec(memory_space=pltpu.VMEM)] * len(args),
        out_specs=pl.BlockSpec(memory_space=pltpu.VMEM),
        out_shape=jax.ShapeDtypeStruct((n, keys.shape[1], w.shape[0] // n), jnp.bfloat16),
        compiler_params=pltpu.CompilerParams(vmem_limit_bytes=VMEM_BYTES),
    )(*args)


def pick(a, i, axis=0):
    return lax.dynamic_index_in_dim(a, i, axis, keepdims=False)


def after(x, *others):
    return lax.optimization_barrier((x,) + others)[0]


def swap(x, axis):
    return lax.all_to_all(x, axis, 0, 0, tiled=True)


def share(x, axis):
    return swap(jnp.broadcast_to(x[None], (lax.axis_size(axis),) + x.shape), axis)


def per_device(
    text, order, lengths, image, in_gain, wq, wk, wv, wo, query_norm_gain, k_gain, gate, cot
):
    D, S, T = lax.axis_size("dp"), lax.axis_size("section"), lax.axis_size("tensor")
    R = T // D
    d, s, t = lax.axis_index("dp"), lax.axis_index("section"), lax.axis_index("tensor")
    slots, rows = text.shape[:2]
    width = in_gain.shape[1]
    hd = k_gain.shape[1]
    feats = width // T
    chunk = feats // D
    toks = image.shape[1] * S

    def onward(x):
        return lax.ppermute(x, "section", [(i, (i + 1) % S) for i in range(S)])

    def dp_flip(x, m):
        return lax.ppermute(x, "dp", [(i, i ^ m) for i in range(D)])

    def dp_all(x):
        across = dp_flip(x, 2)
        return [x, dp_flip(x, 1), across, dp_flip(across, 1)]

    def spread(x):
        a, c = t // R, t % D
        parts = jnp.stack(jnp.split(x, D, axis=-1))
        got = []
        for k in range(D):
            pairs = [(i * R + b, b * D + (i + k) % D) for i in range(D) for b in range(R)]
            got.append(lax.ppermute(pick(parts, (a + k) % D), "tensor", pairs))
        got = jnp.stack(got)
        return jnp.concatenate([pick(got, (c - (d ^ j)) % D) for j in range(D)], axis=-1)

    def unspread(x):
        a, c = t // R, t % D
        parts = jnp.stack(jnp.split(x, D, axis=-1))
        got = []
        for k in range(D):
            pairs = [(b * D + (i + k) % D, i * R + b) for i in range(D) for b in range(R)]
            got.append(lax.ppermute(pick(parts, ((c - k) % D) ^ d), "tensor", pairs))
        got = jnp.stack(got)
        return jnp.concatenate([pick(got, (j - a) % D) for j in range(D)], axis=-1)

    micro = order[0]
    lens = jnp.take(lengths[0], micro)
    alpha = jnp.tanh(gate)

    shared = share(jnp.take(image, micro, axis=0).reshape(-1, feats), "section")
    img = lax.all_gather(shared.reshape(slots * toks, feats), "tensor", axis=1, tiled=True)
    wkv = jnp.concatenate([wk[0], wv[0]], axis=1)
    wkv = lax.all_gather(wkv, "dp", axis=0, tiled=True)
    kv = jnp.dot(img, wkv, preferred_element_type=jnp.float32)
    kv = jnp.moveaxis(kv.reshape(S, slots, toks // S, 2 * hd), 0, 1).reshape(slots, toks, 2 * hd)
    k_raw, vals = kv[..., :hd], kv[..., hd:]
    keys = k_raw * lax.rsqrt(jnp.mean(k_raw * k_raw, axis=-1, keepdims=True) + EPS) * k_gain[0]

    wq_own = swap(after(wq[0].reshape(T, chunk, wq.shape[2]), shared), "tensor")
    wq_f = dp_all(wq_own)
    text_f = spread(after(jnp.take(text, micro, axis=0), shared))
    gain_f = pick(in_gain.reshape(D, T, chunk), t, 1)
    gain_f = jnp.concatenate([pick(gain_f, d ^ j) for j in range(D)])[None]
    wo_own = jnp.moveaxis(wo[0].reshape(wo.shape[1], T, chunk), 1, 0)
    wo_own = after(wo_own, wq_own, wkv, img, text_f)
    half = wo_own.shape[1] // 2
    wo_a = swap(wo_own[:, :half], "tensor")
    wo_b = swap(after(wo_own[:, half:], wo_a), "tensor")
    ints = jnp.concatenate([s.astype(jnp.int32)[None], lens])

    h = kept_qn = kept_h = None
    grads = []

    def image_part(slot):
        part = back(slot, T, kept_qn, keys, vals, k_raw, d_attn, k_gain, wkv)
        return jnp.sum(swap(part, "tensor").astype(jnp.float32), axis=0).astype(jnp.bfloat16)

    for step in range(S + slots - 1):
        parts, hq = query(step, ints, text_f, gain_f, h, wq_f)
        swapped = swap(parts, "tensor")
        p, kept_qn = attend(step, ints, alpha, width, query_norm_gain, keys, swapped, kept_qn)
        if step == 0:
            vals16 = vals.astype(jnp.bfloat16).reshape(slots * toks, hd)
            vals16 = jnp.broadcast_to(vals16[None], (T,) + vals16.shape)
            both = swap(jnp.concatenate([p, vals16], axis=1), "tensor")
            probs = both[:, :rows]
            wo_f = []
            for own in (wo_a, wo_b):
                across = dp_flip(own, 2)
                wo_f += [own, dp_flip(own, 1), across, dp_flip(after(across, probs), 1)]
            vo = value_out(both[:, rows:], wo_f, slots)
        else:
            probs = swap(after(p, *grads), "tensor")
        if step == 1:
            wo_full = lax.all_gather(after(wo[0], p), "dp", axis=1, tiled=True)
        if step == 5:
            mask = (jnp.arange(rows)[None, :] < lens[:, None]).astype(jnp.float32)[:, :, None]
            d_attn = dot16(cot[0].reshape(slots * rows, width), wo_full, ROWS_ROWS)
            d_attn = alpha[0] * mask * d_attn.reshape(slots, rows, -1)
            probs, d_attn = lax.optimization_barrier((probs, d_attn))
        if step >= S - 1:
            grads.append(image_part(step - S + 1))
        h, kept_h = output(step, ints, probs, vo, hq, kept_h)
        h = onward(h)

    states = unspread(kept_h)
    grad = jnp.stack(grads).reshape(slots, S, toks // S, feats)
    grad = swap(jnp.moveaxis(grad, 1, 0), "section")
    grad = jnp.sum(grad.astype(jnp.float32), axis=0)
    grad = jnp.stack([pick(grad, jnp.argmax(micro == m)) for m in range(slots)])
    return (states[None], grad)


def solution(mesh):
    return jax.shard_map(
        per_device,
        mesh=mesh,
        in_specs=(
            P("dp", None, "tensor"),
            P("dp", None),
            P("dp", None),
            P("dp", "section", "tensor"),
            P("section", None),
            P("section", "dp", "tensor"),
            P("section", "dp", "tensor"),
            P("section", "dp", "tensor"),
            P("section", "tensor", "dp"),
            P("section", None),
            P("section", None),
            P("section"),
            P("section", "dp", None, None),
        ),
        out_specs=(P("section", "dp", None, "tensor"), P("dp", "section", "tensor")),
        check_vma=False,
    )
```

```python
import functools
import math

import jax
import jax.numpy as jnp
from jax import lax
from jax.experimental import pallas as pl
from jax.experimental.pallas import tpu as pltpu
from jax.sharding import PartitionSpec as P

EPS = 1e-05
HIGH = lax.Precision.HIGHEST
LANES = 128
EXTRA = 16
VMEM_BYTES = 14 * 2**20
ROWS_ROWS = (((1,), (1,)), ((), ()))
COLS_COLS = (((0,), (0,)), ((), ()))


def dot32(a, b, dims=(((1,), (0,)), ((), ()))):
    return lax.dot_general(a, b, dims, precision=HIGH, preferred_element_type=jnp.float32)


def dot16(a, b, dims=(((1,), (0,)), ((), ()))):
    return lax.dot_general(a, b, dims, preferred_element_type=jnp.float32)


def slot_of(step, ints, slots):
    return jnp.clip(step - ints[0], 0, slots - 1)


def query_kernel(step, ints, text_ref, gain_ref, *refs):
    h_ref = refs[0] if len(refs) == 9 else None
    w_refs, q_ref, hq_ref, w_s, sems = refs[-8:-4], refs[-4], refs[-3], refs[-2], refs[-1]
    n, chunk, cols = w_refs[0].shape
    copies = []
    for half in range(2):
        at = pl.ds(half * (n // 2), n // 2)
        for j in range(4):
            copy = pltpu.make_async_copy(w_refs[j].at[at], w_s.at[j, at], sems.at[half, j])
            copy.start()
            copies.append(copy)
    h = text_ref[slot_of(step, ints, text_ref.shape[0])]
    if h_ref is not None:
        h = jnp.where(ints[0] == 0, h, h_ref[...])
    hq_ref[...] = h
    hf = h.astype(jnp.float32)
    x = (hf * gain_ref[...]).astype(jnp.bfloat16)
    ss = jnp.sum(hf * hf, axis=1, keepdims=True)
    hi = ss.astype(jnp.bfloat16).astype(jnp.float32)
    rows = h.shape[0]
    own, lane = own_lanes(rows)
    pair = jnp.where(own, jnp.where(lane < rows, hi, ss - hi), 0.0)
    pair = jnp.broadcast_to(jnp.sum(pair, axis=0, keepdims=True), (EXTRA, LANES))
    pair = pair.astype(jnp.bfloat16)
    for k in range(n):
        if k % (n // 2) == 0:
            for copy in copies[k // (n // 2) * 4 :][:4]:
                copy.wait()
        acc = dot16(x[:, :chunk], w_s[0, k])
        for j in range(1, 4):
            acc += dot16(x[:, j * chunk : (j + 1) * chunk], w_s[j, k])
        acc = acc.astype(jnp.bfloat16)
        for i in range(cols // LANES):
            q_ref[k, i * rows : (i + 1) * rows, :] = acc[:, i * LANES : (i + 1) * LANES]
        q_ref[k, cols // LANES * rows :, :] = pair


def query(step, ints, text, gain, h, w):
    rows, feats = text.shape[1:]
    n, chunk, cols = w[0].shape
    args = [text, gain] + ([] if h is None else [h])
    return pl.pallas_call(
        functools.partial(query_kernel, step),
        in_specs=[pl.BlockSpec(memory_space=pltpu.SMEM)]
        + [pl.BlockSpec(memory_space=pltpu.VMEM)] * len(args)
        + [pl.BlockSpec(memory_space=pl.ANY)] * 4,
        out_specs=[pl.BlockSpec(memory_space=pltpu.VMEM)] * 2,
        out_shape=[
            jax.ShapeDtypeStruct((n, cols // LANES * rows + EXTRA, LANES), jnp.bfloat16),
            jax.ShapeDtypeStruct((rows, feats), jnp.bfloat16),
        ],
        scratch_shapes=[
            pltpu.VMEM((4, n, chunk, cols), jnp.bfloat16),
            pltpu.SemaphoreType.DMA((2, 4)),
        ],
        compiler_params=pltpu.CompilerParams(vmem_limit_bytes=VMEM_BYTES),
    )(ints, *args, *w)


def keep(step, ints, kept_ref, new, old_ref):
    for o in range(kept_ref.shape[0]):
        old = jnp.zeros(new.shape, new.dtype) if old_ref is None else old_ref[o]
        kept_ref[o] = jnp.where(step - ints[0] == o, new, old)


def output_kernel(step, ints, p_ref, vo_ref, h_ref, *refs):
    o_ref, kept_ref = refs[-2:]
    probs = jnp.concatenate([p_ref[i] for i in range(p_ref.shape[0])], axis=1)
    new = h_ref[...].astype(jnp.float32) + dot16(probs, vo_ref[slot_of(step, ints, vo_ref.shape[0])])
    new = new.astype(jnp.bfloat16)
    o_ref[...] = new
    keep(step, ints, kept_ref, new, refs[0] if len(refs) == 3 else None)


def output(step, ints, probs, vo, h, kept):
    args = [probs, vo, h] + ([] if kept is None else [kept])
    return pl.pallas_call(
        functools.partial(output_kernel, step),
        in_specs=[pl.BlockSpec(memory_space=pltpu.SMEM)]
        + [pl.BlockSpec(memory_space=pltpu.VMEM)] * len(args),
        out_specs=[pl.BlockSpec(memory_space=pltpu.VMEM)] * 2,
        out_shape=[
            jax.ShapeDtypeStruct(h.shape, jnp.bfloat16),
            jax.ShapeDtypeStruct(vo.shape[:1] + h.shape, jnp.bfloat16),
        ],
        compiler_params=pltpu.CompilerParams(vmem_limit_bytes=VMEM_BYTES),
    )(ints, *args)


def own_lanes(rows):
    row = lax.broadcasted_iota(jnp.int32, (rows, LANES), 0)
    lane = lax.broadcasted_iota(jnp.int32, (rows, LANES), 1)
    return (lane == row) | (lane == row + rows), lane


def whole(shape):
    return pl.BlockSpec(shape, lambda *_: (0,) * len(shape))


def attend_kernel(step, width, ints, alpha_ref, gain_ref, k_ref, q_ref, *refs):
    p_ref, kept_ref = refs[-2:]
    slot = slot_of(step, ints, k_ref.shape[0])
    total = q_ref[0].astype(jnp.float32)
    for i in range(1, q_ref.shape[0]):
        total += q_ref[i].astype(jnp.float32)
    hd = gain_ref.shape[1]
    rows, cols = kept_ref.shape[1:]
    own, _ = own_lanes(rows)
    sums = jnp.broadcast_to(total[cols // hd * rows : cols // hd * rows + 1], (rows, LANES))
    ss = jnp.sum(jnp.where(own, sums, 0.0), axis=1, keepdims=True)
    rs = lax.rsqrt(ss / width + EPS)
    keys = k_ref[slot]
    row = lax.broadcasted_iota(jnp.int32, (rows, keys.shape[0]), 0)
    scale = jnp.where(row < ints[1 + slot], alpha_ref[0], 0.0)
    parts, normed = [], []
    for h in range(cols // hd):
        q = total[h * rows : (h + 1) * rows] * rs
        r = lax.rsqrt(jnp.mean(q * q, axis=1, keepdims=True) + EPS)
        qn = q * r * gain_ref[...] * (1.0 / math.sqrt(hd))
        normed.append(qn)
        sc = dot32(qn, keys, ROWS_ROWS)
        e = jnp.exp(sc - jnp.max(sc, axis=1, keepdims=True))
        parts.append(scale * e / jnp.sum(e, axis=1, keepdims=True))
    p = jnp.concatenate(parts, axis=1).astype(jnp.bfloat16)
    for i in range(p_ref.shape[0]):
        p_ref[i] = p
    old_ref = refs[0] if len(refs) == 3 else None
    keep(step, ints, kept_ref, jnp.concatenate(normed, axis=1), old_ref)


def attend(step, ints, alpha, width, gain, keys, parts, kept):
    hd = gain.shape[1]
    toks = keys.shape[1]
    heads = 4
    n = parts.shape[0]
    rows = (parts.shape[1] - EXTRA) // heads
    args = [gain, keys, parts] + ([] if kept is None else [kept])
    return pl.pallas_call(
        functools.partial(attend_kernel, step, width),
        in_specs=[pl.BlockSpec(memory_space=pltpu.SMEM)] * 2
        + [pl.BlockSpec(memory_space=pltpu.VMEM)] * len(args),
        out_specs=[pl.BlockSpec(memory_space=pltpu.VMEM)] * 2,
        out_shape=[
            jax.ShapeDtypeStruct((n, rows, heads * toks), jnp.bfloat16),
            jax.ShapeDtypeStruct(keys.shape[:1] + (rows, heads * hd), jnp.float32),
        ],
        compiler_params=pltpu.CompilerParams(vmem_limit_bytes=VMEM_BYTES),
    )(ints, alpha, *args)


def value_out_kernel(slots, v_ref, *refs):
    w_refs, o_ref = refs[:-1], refs[-1]
    n, vrows, hd = v_ref.shape
    toks = vrows // slots
    part, chunk = w_refs[0].shape[1] // hd, w_refs[0].shape[2]
    heads = part * len(w_refs) // 4

    def block(k, carry):
        v = v_ref[k]
        for h in range(heads):
            at = pl.multiple_of((k * heads + h) * toks, toks)
            for j in range(4):
                w_ref = w_refs[h // part * 4 + j]
                i = h % part * hd
                r = dot16(v, w_ref[k, i : i + hd, :]).astype(jnp.bfloat16)
                for o in range(slots):
                    o_ref[o, pl.ds(at, toks), j * chunk : (j + 1) * chunk] = r[
                        o * toks : (o + 1) * toks
                    ]
        return carry

    lax.fori_loop(0, n, block, 0)


def value_out(v, w, slots):
    n, vrows, hd = v.shape
    heads = w[0].shape[1] * len(w) // 4 // hd
    chunk = w[0].shape[2]
    toks = vrows // slots
    return pl.pallas_call(
        functools.partial(value_out_kernel, slots),
        in_specs=[pl.BlockSpec(memory_space=pltpu.VMEM)] * (1 + len(w)),
        out_specs=pl.BlockSpec(memory_space=pltpu.VMEM),
        out_shape=jax.ShapeDtypeStruct((slots, n * heads * toks, 4 * chunk), jnp.bfloat16),
        compiler_params=pltpu.CompilerParams(vmem_limit_bytes=VMEM_BYTES),
    )(v, *w)


def back_kernel(slot, qn_ref, k_ref, v_ref, raw_ref, da_ref, gain_ref, w_ref, o_ref):
    keys, vals, raw, gain = k_ref[slot], v_ref[slot], raw_ref[slot], gain_ref[...]
    hd = keys.shape[1]
    d_kn = jnp.zeros(keys.shape, jnp.float32)
    d_v = jnp.zeros(keys.shape, jnp.float32)
    for h in range(qn_ref.shape[2] // hd):
        qn = qn_ref[slot, :, h * hd : (h + 1) * hd]
        da = da_ref[slot, :, h * hd : (h + 1) * hd]
        sc = dot32(qn, keys, ROWS_ROWS)
        e = jnp.exp(sc - jnp.max(sc, axis=1, keepdims=True))
        p = e / jnp.sum(e, axis=1, keepdims=True)
        dp = dot32(da, vals, ROWS_ROWS)
        ds = p * (dp - jnp.sum(p * dp, axis=1, keepdims=True))
        d_kn += dot32(ds, qn, COLS_COLS)
        d_v += dot32(p, da, COLS_COLS)
    r = lax.rsqrt(jnp.mean(raw * raw, axis=1, keepdims=True) + EPS)
    u = d_kn * gain
    d_k = r * u - raw * (r * r * r * jnp.mean(raw * u, axis=1, keepdims=True))
    d_kv = jnp.concatenate([d_k, d_v], axis=1).astype(jnp.bfloat16)
    feats = o_ref.shape[2]
    for i in range(o_ref.shape[0]):
        part = dot16(d_kv, w_ref[i * feats : (i + 1) * feats], ROWS_ROWS)
        o_ref[i] = part.astype(jnp.bfloat16)


def back(slot, n, qn, keys, vals, raw, da, gain, w):
    args = (qn, keys, vals, raw, da, gain, w)
    return pl.pallas_call(
        functools.partial(back_kernel, slot),
        in_specs=[pl.BlockSpec(memory_space=pltpu.VMEM)] * len(args),
        out_specs=pl.BlockSpec(memory_space=pltpu.VMEM),
        out_shape=jax.ShapeDtypeStruct((n, keys.shape[1], w.shape[0] // n), jnp.bfloat16),
        compiler_params=pltpu.CompilerParams(vmem_limit_bytes=VMEM_BYTES),
    )(*args)


def pick(a, i, axis=0):
    return lax.dynamic_index_in_dim(a, i, axis, keepdims=False)


def after(x, *others):
    return lax.optimization_barrier((x,) + others)[0]


def swap(x, axis):
    return lax.all_to_all(x, axis, 0, 0, tiled=True)


def share(x, axis):
    return swap(jnp.broadcast_to(x[None], (lax.axis_size(axis),) + x.shape), axis)


def per_device(
    text, order, lengths, image, in_gain, wq, wk, wv, wo, query_norm_gain, k_gain, gate, cot
):
    D, S, T = lax.axis_size("dp"), lax.axis_size("section"), lax.axis_size("tensor")
    R = T // D
    d, s, t = lax.axis_index("dp"), lax.axis_index("section"), lax.axis_index("tensor")
    slots, rows = text.shape[:2]
    width = in_gain.shape[1]
    hd = k_gain.shape[1]
    feats = width // T
    chunk = feats // D
    toks = image.shape[1] * S

    def onward(x):
        return lax.ppermute(x, "section", [(i, (i + 1) % S) for i in range(S)])

    def dp_flip(x, m):
        return lax.ppermute(x, "dp", [(i, i ^ m) for i in range(D)])

    def dp_all(x):
        across = dp_flip(x, 2)
        return [x, dp_flip(x, 1), across, dp_flip(across, 1)]

    def spread(x):
        a, c = t // R, t % D
        parts = jnp.stack(jnp.split(x, D, axis=-1))
        got = []
        for k in range(D):
            pairs = [(i * R + b, b * D + (i + k) % D) for i in range(D) for b in range(R)]
            got.append(lax.ppermute(pick(parts, (a + k) % D), "tensor", pairs))
        got = jnp.stack(got)
        return jnp.concatenate([pick(got, (c - (d ^ j)) % D) for j in range(D)], axis=-1)

    def unspread(x):
        a, c = t // R, t % D
        parts = jnp.stack(jnp.split(x, D, axis=-1))
        got = []
        for k in range(D):
            pairs = [(b * D + (i + k) % D, i * R + b) for i in range(D) for b in range(R)]
            got.append(lax.ppermute(pick(parts, ((c - k) % D) ^ d), "tensor", pairs))
        got = jnp.stack(got)
        return jnp.concatenate([pick(got, (j - a) % D) for j in range(D)], axis=-1)

    micro = order[0]
    lens = jnp.take(lengths[0], micro)
    alpha = jnp.tanh(gate)

    wkv = jnp.concatenate([wk[0], wv[0]], axis=1)
    shared = share(after(jnp.take(image, micro, axis=0), wkv).reshape(-1, feats), "section")
    wkv = lax.all_gather(wkv, "dp", axis=0, tiled=True)

    wq_own = swap(after(wq[0].reshape(T, chunk, wq.shape[2]), shared), "tensor")
    wq_f = dp_all(wq_own)
    text_f = spread(after(jnp.take(text, micro, axis=0), shared))
    img = after(shared, wq_own).reshape(slots * toks, feats)
    img = lax.all_gather(img, "tensor", axis=1, tiled=True)
    gain_f = pick(in_gain.reshape(D, T, chunk), t, 1)
    gain_f = jnp.concatenate([pick(gain_f, d ^ j) for j in range(D)])[None]
    wo_own = jnp.moveaxis(wo[0].reshape(wo.shape[1], T, chunk), 1, 0)
    wo_own = after(wo_own, wq_own, wkv, text_f)
    half = wo_own.shape[1] // 2
    wo_a = swap(wo_own[:, :half], "tensor")
    wo_b = swap(after(wo_own[:, half:], wo_a, img), "tensor")
    kv = jnp.dot(img, wkv, preferred_element_type=jnp.float32)
    kv = jnp.moveaxis(kv.reshape(S, slots, toks // S, 2 * hd), 0, 1).reshape(slots, toks, 2 * hd)
    k_raw, vals = kv[..., :hd], kv[..., hd:]
    keys = k_raw * lax.rsqrt(jnp.mean(k_raw * k_raw, axis=-1, keepdims=True) + EPS) * k_gain[0]
    ints = jnp.concatenate([s.astype(jnp.int32)[None], lens])

    h = kept_qn = kept_h = None
    grads = []

    def image_part(slot):
        part = back(slot, T, kept_qn, keys, vals, k_raw, d_attn, k_gain, wkv)
        return jnp.sum(swap(part, "tensor").astype(jnp.float32), axis=0).astype(jnp.bfloat16)

    for step in range(S + slots - 1):
        parts, hq = query(step, ints, text_f, gain_f, h, wq_f)
        swapped = swap(parts, "tensor")
        p, kept_qn = attend(step, ints, alpha, width, query_norm_gain, keys, swapped, kept_qn)
        if step == 0:
            vals16 = vals.astype(jnp.bfloat16).reshape(slots * toks, hd)
            vals16 = jnp.broadcast_to(vals16[None], (T,) + vals16.shape)
            both = swap(jnp.concatenate([p, vals16], axis=1), "tensor")
            probs = both[:, :rows]
            wo_f = []
            for own in (wo_a, wo_b):
                across = dp_flip(own, 2)
                wo_f += [own, dp_flip(own, 1), across, dp_flip(after(across, probs), 1)]
            vo = value_out(both[:, rows:], wo_f, slots)
        else:
            probs = swap(after(p, *grads), "tensor")
        if step == 1:
            wo_full = lax.all_gather(after(wo[0], p), "dp", axis=1, tiled=True)
        if step == 5:
            mask = (jnp.arange(rows)[None, :] < lens[:, None]).astype(jnp.float32)[:, :, None]
            d_attn = dot16(cot[0].reshape(slots * rows, width), wo_full, ROWS_ROWS)
            d_attn = alpha[0] * mask * d_attn.reshape(slots, rows, -1)
            probs, d_attn = lax.optimization_barrier((probs, d_attn))
        if step >= S - 1:
            grads.append(image_part(step - S + 1))
        h, kept_h = output(step, ints, probs, vo, hq, kept_h)
        h = onward(h)

    states = unspread(kept_h)
    grad = jnp.stack(grads).reshape(slots, S, toks // S, feats)
    grad = swap(jnp.moveaxis(grad, 1, 0), "section")
    grad = jnp.sum(grad.astype(jnp.float32), axis=0)
    grad = jnp.stack([pick(grad, jnp.argmax(micro == m)) for m in range(slots)])
    return (states[None], grad)


def solution(mesh):
    return jax.shard_map(
        per_device,
        mesh=mesh,
        in_specs=(
            P("dp", None, "tensor"),
            P("dp", None),
            P("dp", None),
            P("dp", "section", "tensor"),
            P("section", None),
            P("section", "dp", "tensor"),
            P("section", "dp", "tensor"),
            P("section", "dp", "tensor"),
            P("section", "tensor", "dp"),
            P("section", None),
            P("section", None),
            P("section"),
            P("section", "dp", None, None),
        ),
        out_specs=(P("section", "dp", None, "tensor"), P("dp", "section", "tensor")),
        check_vma=False,
    )
```

```python
import functools
import math

import jax
import jax.numpy as jnp
from jax import lax
from jax.experimental import pallas as pl
from jax.experimental.pallas import tpu as pltpu
from jax.sharding import PartitionSpec as P

EPS = 1e-05
HIGH = lax.Precision.HIGHEST
LANES = 128
EXTRA = 16
VMEM_BYTES = 14 * 2**20
ROWS_ROWS = (((1,), (1,)), ((), ()))
COLS_COLS = (((0,), (0,)), ((), ()))


def dot32(a, b, dims=(((1,), (0,)), ((), ()))):
    return lax.dot_general(a, b, dims, precision=HIGH, preferred_element_type=jnp.float32)


def dot16(a, b, dims=(((1,), (0,)), ((), ()))):
    return lax.dot_general(a, b, dims, preferred_element_type=jnp.float32)


def slot_of(step, ints, slots):
    return jnp.clip(step - ints[0], 0, slots - 1)


def query_kernel(step, ints, text_ref, gain_ref, *refs):
    h_ref = refs[0] if len(refs) == 9 else None
    w_refs, q_ref, hq_ref, w_s, sems = refs[-8:-4], refs[-4], refs[-3], refs[-2], refs[-1]
    n, chunk, cols = w_refs[0].shape
    copies = []
    for half in range(2):
        at = pl.ds(half * (n // 2), n // 2)
        for j in range(4):
            copy = pltpu.make_async_copy(w_refs[j].at[at], w_s.at[j, at], sems.at[half, j])
            copy.start()
            copies.append(copy)
    h = text_ref[slot_of(step, ints, text_ref.shape[0])]
    if h_ref is not None:
        h = jnp.where(ints[0] == 0, h, h_ref[...])
    hq_ref[...] = h
    hf = h.astype(jnp.float32)
    x = (hf * gain_ref[...]).astype(jnp.bfloat16)
    ss = jnp.sum(hf * hf, axis=1, keepdims=True)
    hi = ss.astype(jnp.bfloat16).astype(jnp.float32)
    rows = h.shape[0]
    own, lane = own_lanes(rows)
    pair = jnp.where(own, jnp.where(lane < rows, hi, ss - hi), 0.0)
    pair = jnp.broadcast_to(jnp.sum(pair, axis=0, keepdims=True), (EXTRA, LANES))
    pair = pair.astype(jnp.bfloat16)
    for k in range(n):
        if k % (n // 2) == 0:
            for copy in copies[k // (n // 2) * 4 :][:4]:
                copy.wait()
        acc = dot16(x[:, :chunk], w_s[0, k])
        for j in range(1, 4):
            acc += dot16(x[:, j * chunk : (j + 1) * chunk], w_s[j, k])
        acc = acc.astype(jnp.bfloat16)
        for i in range(cols // LANES):
            q_ref[k, i * rows : (i + 1) * rows, :] = acc[:, i * LANES : (i + 1) * LANES]
        q_ref[k, cols // LANES * rows :, :] = pair


def query(step, ints, text, gain, h, w):
    rows, feats = text.shape[1:]
    n, chunk, cols = w[0].shape
    args = [text, gain] + ([] if h is None else [h])
    return pl.pallas_call(
        functools.partial(query_kernel, step),
        in_specs=[pl.BlockSpec(memory_space=pltpu.SMEM)]
        + [pl.BlockSpec(memory_space=pltpu.VMEM)] * len(args)
        + [pl.BlockSpec(memory_space=pl.ANY)] * 4,
        out_specs=[pl.BlockSpec(memory_space=pltpu.VMEM)] * 2,
        out_shape=[
            jax.ShapeDtypeStruct((n, cols // LANES * rows + EXTRA, LANES), jnp.bfloat16),
            jax.ShapeDtypeStruct((rows, feats), jnp.bfloat16),
        ],
        scratch_shapes=[
            pltpu.VMEM((4, n, chunk, cols), jnp.bfloat16),
            pltpu.SemaphoreType.DMA((2, 4)),
        ],
        compiler_params=pltpu.CompilerParams(vmem_limit_bytes=VMEM_BYTES),
    )(ints, *args, *w)


def keep(step, ints, kept_ref, new, old_ref):
    for o in range(kept_ref.shape[0]):
        old = jnp.zeros(new.shape, new.dtype) if old_ref is None else old_ref[o]
        kept_ref[o] = jnp.where(step - ints[0] == o, new, old)


def output_kernel(step, ints, p_ref, vo_ref, h_ref, *refs):
    o_ref, kept_ref = refs[-2:]
    probs = jnp.concatenate([p_ref[i] for i in range(p_ref.shape[0])], axis=1)
    new = h_ref[...].astype(jnp.float32) + dot16(probs, vo_ref[slot_of(step, ints, vo_ref.shape[0])])
    new = new.astype(jnp.bfloat16)
    o_ref[...] = new
    keep(step, ints, kept_ref, new, refs[0] if len(refs) == 3 else None)


def output(step, ints, probs, vo, h, kept):
    args = [probs, vo, h] + ([] if kept is None else [kept])
    return pl.pallas_call(
        functools.partial(output_kernel, step),
        in_specs=[pl.BlockSpec(memory_space=pltpu.SMEM)]
        + [pl.BlockSpec(memory_space=pltpu.VMEM)] * len(args),
        out_specs=[pl.BlockSpec(memory_space=pltpu.VMEM)] * 2,
        out_shape=[
            jax.ShapeDtypeStruct(h.shape, jnp.bfloat16),
            jax.ShapeDtypeStruct(vo.shape[:1] + h.shape, jnp.bfloat16),
        ],
        compiler_params=pltpu.CompilerParams(vmem_limit_bytes=VMEM_BYTES),
    )(ints, *args)


def own_lanes(rows):
    row = lax.broadcasted_iota(jnp.int32, (rows, LANES), 0)
    lane = lax.broadcasted_iota(jnp.int32, (rows, LANES), 1)
    return (lane == row) | (lane == row + rows), lane


def whole(shape):
    return pl.BlockSpec(shape, lambda *_: (0,) * len(shape))


def attend_kernel(step, width, ints, alpha_ref, gain_ref, k_ref, q_ref, *refs):
    p_ref, kept_ref = refs[-2:]
    slot = slot_of(step, ints, k_ref.shape[0])
    total = q_ref[0].astype(jnp.float32)
    for i in range(1, q_ref.shape[0]):
        total += q_ref[i].astype(jnp.float32)
    hd = gain_ref.shape[1]
    rows, cols = kept_ref.shape[1:]
    own, _ = own_lanes(rows)
    sums = jnp.broadcast_to(total[cols // hd * rows : cols // hd * rows + 1], (rows, LANES))
    ss = jnp.sum(jnp.where(own, sums, 0.0), axis=1, keepdims=True)
    rs = lax.rsqrt(ss / width + EPS)
    keys = k_ref[slot]
    row = lax.broadcasted_iota(jnp.int32, (rows, keys.shape[0]), 0)
    scale = jnp.where(row < ints[1 + slot], alpha_ref[0], 0.0)
    parts, normed = [], []
    for h in range(cols // hd):
        q = total[h * rows : (h + 1) * rows] * rs
        r = lax.rsqrt(jnp.mean(q * q, axis=1, keepdims=True) + EPS)
        qn = q * r * gain_ref[...] * (1.0 / math.sqrt(hd))
        normed.append(qn)
        sc = dot32(qn, keys, ROWS_ROWS)
        e = jnp.exp(sc - jnp.max(sc, axis=1, keepdims=True))
        parts.append(scale * e / jnp.sum(e, axis=1, keepdims=True))
    p = jnp.concatenate(parts, axis=1).astype(jnp.bfloat16)
    for i in range(p_ref.shape[0]):
        p_ref[i] = p
    old_ref = refs[0] if len(refs) == 3 else None
    keep(step, ints, kept_ref, jnp.concatenate(normed, axis=1), old_ref)


def attend(step, ints, alpha, width, gain, keys, parts, kept):
    hd = gain.shape[1]
    toks = keys.shape[1]
    heads = 4
    n = parts.shape[0]
    rows = (parts.shape[1] - EXTRA) // heads
    args = [gain, keys, parts] + ([] if kept is None else [kept])
    return pl.pallas_call(
        functools.partial(attend_kernel, step, width),
        in_specs=[pl.BlockSpec(memory_space=pltpu.SMEM)] * 2
        + [pl.BlockSpec(memory_space=pltpu.VMEM)] * len(args),
        out_specs=[pl.BlockSpec(memory_space=pltpu.VMEM)] * 2,
        out_shape=[
            jax.ShapeDtypeStruct((n, rows, heads * toks), jnp.bfloat16),
            jax.ShapeDtypeStruct(keys.shape[:1] + (rows, heads * hd), jnp.float32),
        ],
        compiler_params=pltpu.CompilerParams(vmem_limit_bytes=VMEM_BYTES),
    )(ints, alpha, *args)


def value_out_kernel(slots, v_ref, *refs):
    w_refs, o_ref = refs[:-1], refs[-1]
    n, vrows, hd = v_ref.shape
    toks = vrows // slots
    part, chunk = w_refs[0].shape[1] // hd, w_refs[0].shape[2]
    heads = part * len(w_refs) // 4

    def block(k, carry):
        v = v_ref[k]
        for h in range(heads):
            at = pl.multiple_of((k * heads + h) * toks, toks)
            for j in range(4):
                w_ref = w_refs[h // part * 4 + j]
                i = h % part * hd
                r = dot16(v, w_ref[k, i : i + hd, :]).astype(jnp.bfloat16)
                for o in range(slots):
                    o_ref[o, pl.ds(at, toks), j * chunk : (j + 1) * chunk] = r[
                        o * toks : (o + 1) * toks
                    ]
        return carry

    lax.fori_loop(0, n, block, 0)


def value_out(v, w, slots):
    n, vrows, hd = v.shape
    heads = w[0].shape[1] * len(w) // 4 // hd
    chunk = w[0].shape[2]
    toks = vrows // slots
    return pl.pallas_call(
        functools.partial(value_out_kernel, slots),
        in_specs=[pl.BlockSpec(memory_space=pltpu.VMEM)] * (1 + len(w)),
        out_specs=pl.BlockSpec(memory_space=pltpu.VMEM),
        out_shape=jax.ShapeDtypeStruct((slots, n * heads * toks, 4 * chunk), jnp.bfloat16),
        compiler_params=pltpu.CompilerParams(vmem_limit_bytes=VMEM_BYTES),
    )(v, *w)


def back_kernel(slot, qn_ref, k_ref, v_ref, raw_ref, da_ref, gain_ref, w_ref, o_ref):
    keys, vals, raw, gain = k_ref[slot], v_ref[slot], raw_ref[slot], gain_ref[...]
    hd = keys.shape[1]
    d_kn = jnp.zeros(keys.shape, jnp.float32)
    d_v = jnp.zeros(keys.shape, jnp.float32)
    for h in range(qn_ref.shape[2] // hd):
        qn = qn_ref[slot, :, h * hd : (h + 1) * hd]
        da = da_ref[slot, :, h * hd : (h + 1) * hd]
        sc = dot32(qn, keys, ROWS_ROWS)
        e = jnp.exp(sc - jnp.max(sc, axis=1, keepdims=True))
        p = e / jnp.sum(e, axis=1, keepdims=True)
        dp = dot32(da, vals, ROWS_ROWS)
        ds = p * (dp - jnp.sum(p * dp, axis=1, keepdims=True))
        d_kn += dot32(ds, qn, COLS_COLS)
        d_v += dot32(p, da, COLS_COLS)
    r = lax.rsqrt(jnp.mean(raw * raw, axis=1, keepdims=True) + EPS)
    u = d_kn * gain
    d_k = r * u - raw * (r * r * r * jnp.mean(raw * u, axis=1, keepdims=True))
    d_kv = jnp.concatenate([d_k, d_v], axis=1).astype(jnp.bfloat16)
    feats = o_ref.shape[2]
    for i in range(o_ref.shape[0]):
        part = dot16(d_kv, w_ref[i * feats : (i + 1) * feats], ROWS_ROWS)
        o_ref[i] = part.astype(jnp.bfloat16)


def back(slot, n, qn, keys, vals, raw, da, gain, w):
    args = (qn, keys, vals, raw, da, gain, w)
    return pl.pallas_call(
        functools.partial(back_kernel, slot),
        in_specs=[pl.BlockSpec(memory_space=pltpu.VMEM)] * len(args),
        out_specs=pl.BlockSpec(memory_space=pltpu.VMEM),
        out_shape=jax.ShapeDtypeStruct((n, keys.shape[1], w.shape[0] // n), jnp.bfloat16),
        compiler_params=pltpu.CompilerParams(vmem_limit_bytes=VMEM_BYTES),
    )(*args)


def pick(a, i, axis=0):
    return lax.dynamic_index_in_dim(a, i, axis, keepdims=False)


def after(x, *others):
    return lax.optimization_barrier((x,) + others)[0]


def swap(x, axis):
    return lax.all_to_all(x, axis, 0, 0, tiled=True)


def share(x, axis):
    return swap(jnp.broadcast_to(x[None], (lax.axis_size(axis),) + x.shape), axis)


def per_device(
    text, order, lengths, image, in_gain, wq, wk, wv, wo, query_norm_gain, k_gain, gate, cot
):
    D, S, T = lax.axis_size("dp"), lax.axis_size("section"), lax.axis_size("tensor")
    R = T // D
    d, s, t = lax.axis_index("dp"), lax.axis_index("section"), lax.axis_index("tensor")
    slots, rows = text.shape[:2]
    width = in_gain.shape[1]
    hd = k_gain.shape[1]
    feats = width // T
    chunk = feats // D
    toks = image.shape[1] * S

    def onward(x):
        return lax.ppermute(x, "section", [(i, (i + 1) % S) for i in range(S)])

    def dp_flip(x, m):
        return lax.ppermute(x, "dp", [(i, i ^ m) for i in range(D)])

    def dp_all(x):
        across = dp_flip(x, 2)
        return [x, dp_flip(x, 1), across, dp_flip(across, 1)]

    def spread(x):
        a, c = t // R, t % D
        parts = jnp.stack(jnp.split(x, D, axis=-1))
        got = []
        for k in range(D):
            pairs = [(i * R + b, b * D + (i + k) % D) for i in range(D) for b in range(R)]
            got.append(lax.ppermute(pick(parts, (a + k) % D), "tensor", pairs))
        got = jnp.stack(got)
        return jnp.concatenate([pick(got, (c - (d ^ j)) % D) for j in range(D)], axis=-1)

    def unspread(x):
        a, c = t // R, t % D
        parts = jnp.stack(jnp.split(x, D, axis=-1))
        got = []
        for k in range(D):
            pairs = [(b * D + (i + k) % D, i * R + b) for i in range(D) for b in range(R)]
            got.append(lax.ppermute(pick(parts, ((c - k) % D) ^ d), "tensor", pairs))
        got = jnp.stack(got)
        return jnp.concatenate([pick(got, (j - a) % D) for j in range(D)], axis=-1)

    micro = order[0]
    lens = jnp.take(lengths[0], micro)
    alpha = jnp.tanh(gate)

    wkv = jnp.concatenate([wk[0], wv[0]], axis=1)
    shared = share(after(jnp.take(image, micro, axis=0), wkv).reshape(-1, feats), "section")
    wkv = lax.all_gather(wkv, "dp", axis=0, tiled=True)

    wq_own = swap(after(wq[0].reshape(T, chunk, wq.shape[2]), shared), "tensor")
    wq_f = dp_all(wq_own)
    text_f = spread(after(jnp.take(text, micro, axis=0), shared))
    img = after(shared, wq_own).reshape(slots * toks, feats)
    img = lax.all_gather(img, "tensor", axis=1, tiled=True)
    gain_f = pick(in_gain.reshape(D, T, chunk), t, 1)
    gain_f = jnp.concatenate([pick(gain_f, d ^ j) for j in range(D)])[None]
    wo_own = jnp.moveaxis(wo[0].reshape(wo.shape[1], T, chunk), 1, 0)
    wo_own = after(wo_own, wq_own, wkv, text_f)
    half = wo_own.shape[1] // 2
    wo_a = swap(wo_own[:, :half], "tensor")
    wo_b = swap(after(wo_own[:, half:], wo_a, img), "tensor")
    kv = jnp.dot(img, wkv, preferred_element_type=jnp.float32)
    kv = jnp.moveaxis(kv.reshape(S, slots, toks // S, 2 * hd), 0, 1).reshape(slots, toks, 2 * hd)
    k_raw, vals = kv[..., :hd], kv[..., hd:]
    keys = k_raw * lax.rsqrt(jnp.mean(k_raw * k_raw, axis=-1, keepdims=True) + EPS) * k_gain[0]
    ints = jnp.concatenate([s.astype(jnp.int32)[None], lens])

    h = kept_qn = kept_h = None
    grads = []

    def image_part(slot):
        part = back(slot, T, kept_qn, keys, vals, k_raw, d_attn, k_gain, wkv)
        return jnp.sum(swap(part, "tensor").astype(jnp.float32), axis=0).astype(jnp.bfloat16)

    for step in range(S + slots - 1):
        parts, hq = query(step, ints, text_f, gain_f, h, wq_f)
        if step == 0:
            across = [dp_flip(own, 2) for own in (wo_a, wo_b)]
            parts = after(parts, across[0])
        swapped = swap(parts, "tensor")
        p, kept_qn = attend(step, ints, alpha, width, query_norm_gain, keys, swapped, kept_qn)
        if step == 0:
            vals16 = vals.astype(jnp.bfloat16).reshape(slots * toks, hd)
            vals16 = jnp.broadcast_to(vals16[None], (T,) + vals16.shape)
            both = swap(jnp.concatenate([after(p, across[1]), vals16], axis=1), "tensor")
            probs = both[:, :rows]
            wo_f = []
            for own, far in zip((wo_a, wo_b), across):
                wo_f += [own, dp_flip(own, 1), far, dp_flip(far, 1)]
            vo = value_out(both[:, rows:], wo_f, slots)
        else:
            probs = swap(after(p, *grads), "tensor")
        if step == 1:
            wo_full = lax.all_gather(after(wo[0], p), "dp", axis=1, tiled=True)
        if step == 5:
            mask = (jnp.arange(rows)[None, :] < lens[:, None]).astype(jnp.float32)[:, :, None]
            d_attn = dot16(cot[0].reshape(slots * rows, width), wo_full, ROWS_ROWS)
            d_attn = alpha[0] * mask * d_attn.reshape(slots, rows, -1)
            probs, d_attn = lax.optimization_barrier((probs, d_attn))
        if step >= S - 1:
            grads.append(image_part(step - S + 1))
        h, kept_h = output(step, ints, probs, vo, hq, kept_h)
        h = onward(h)

    states = unspread(kept_h)
    grad = jnp.stack(grads).reshape(slots, S, toks // S, feats)
    grad = swap(jnp.moveaxis(grad, 1, 0), "section")
    grad = jnp.sum(grad.astype(jnp.float32), axis=0)
    grad = jnp.stack([pick(grad, jnp.argmax(micro == m)) for m in range(slots)])
    return (states[None], grad)


def solution(mesh):
    return jax.shard_map(
        per_device,
        mesh=mesh,
        in_specs=(
            P("dp", None, "tensor"),
            P("dp", None),
            P("dp", None),
            P("dp", "section", "tensor"),
            P("section", None),
            P("section", "dp", "tensor"),
            P("section", "dp", "tensor"),
            P("section", "dp", "tensor"),
            P("section", "tensor", "dp"),
            P("section", None),
            P("section", None),
            P("section"),
            P("section", "dp", None, None),
        ),
        out_specs=(P("section", "dp", None, "tensor"), P("dp", "section", "tensor")),
        check_vma=False,
    )
```

```python
import functools
import math

import jax
import jax.numpy as jnp
from jax import lax
from jax.experimental import pallas as pl
from jax.experimental.pallas import tpu as pltpu
from jax.sharding import PartitionSpec as P

EPS = 1e-05
HIGH = lax.Precision.HIGHEST
LANES = 128
EXTRA = 16
VMEM_BYTES = 14 * 2**20
ROWS_ROWS = (((1,), (1,)), ((), ()))
COLS_COLS = (((0,), (0,)), ((), ()))


def dot32(a, b, dims=(((1,), (0,)), ((), ()))):
    return lax.dot_general(a, b, dims, precision=HIGH, preferred_element_type=jnp.float32)


def dot16(a, b, dims=(((1,), (0,)), ((), ()))):
    return lax.dot_general(a, b, dims, preferred_element_type=jnp.float32)


def slot_of(step, ints, slots):
    return jnp.clip(step - ints[0], 0, slots - 1)


def fetch_kernel(*refs):
    ints, srcs, dst, sems = refs[0], refs[1:-2], refs[-2], refs[-1]
    copies = []
    for i in range(len(srcs)):
        size = srcs[i].shape[0] // 2
        for half in range(2):
            at = pl.ds(half * size, size)
            copies.append(pltpu.make_async_copy(srcs[i].at[at], dst.at[i, at], sems.at[i, half]))
            copies[-1].start()
    for copy in copies:
        copy.wait()


def fetch(ints, arrays):
    return pl.pallas_call(
        fetch_kernel,
        in_specs=[pl.BlockSpec(memory_space=pltpu.SMEM)]
        + [pl.BlockSpec(memory_space=pl.ANY)] * len(arrays),
        out_specs=pl.BlockSpec(memory_space=pltpu.VMEM),
        out_shape=pltpu.VMEM((len(arrays),) + arrays[0].shape, arrays[0].dtype),
        scratch_shapes=[pltpu.SemaphoreType.DMA((len(arrays), 2))],
        compiler_params=pltpu.CompilerParams(vmem_limit_bytes=VMEM_BYTES),
    )(ints, *arrays)


def query_kernel(step, ints, text_ref, gain_ref, *refs):
    copies = []
    if step == 0:
        w_refs, (q_ref, hq_ref, w_s, sems) = refs[:4], refs[4:]
        n = w_s.shape[1]
        for half in range(2):
            at = pl.ds(half * (n // 2), n // 2)
            for j in range(4):
                copy = pltpu.make_async_copy(w_refs[j].at[at], w_s.at[j, at], sems.at[half, j])
                copy.start()
                copies.append(copy)
    else:
        h_ref, w_s, q_ref, hq_ref = refs
    _, n, chunk, cols = w_s.shape
    h = text_ref[slot_of(step, ints, text_ref.shape[0])]
    if step > 0:
        h = jnp.where(ints[0] == 0, h, h_ref[...])
    hq_ref[...] = h
    hf = h.astype(jnp.float32)
    x = (hf * gain_ref[...]).astype(jnp.bfloat16)
    ss = jnp.sum(hf * hf, axis=1, keepdims=True)
    hi = ss.astype(jnp.bfloat16).astype(jnp.float32)
    rows = h.shape[0]
    own, lane = own_lanes(rows)
    pair = jnp.where(own, jnp.where(lane < rows, hi, ss - hi), 0.0)
    pair = jnp.broadcast_to(jnp.sum(pair, axis=0, keepdims=True), (EXTRA, LANES))
    pair = pair.astype(jnp.bfloat16)
    for k in range(n):
        if k % (n // 2) == 0:
            for copy in copies[k // (n // 2) * 4 :][:4]:
                copy.wait()
        acc = dot16(x[:, :chunk], w_s[0, k])
        for j in range(1, 4):
            acc += dot16(x[:, j * chunk : (j + 1) * chunk], w_s[j, k])
        acc = acc.astype(jnp.bfloat16)
        for i in range(cols // LANES):
            q_ref[k, i * rows : (i + 1) * rows, :] = acc[:, i * LANES : (i + 1) * LANES]
        q_ref[k, cols // LANES * rows :, :] = pair


def query(step, ints, text, gain, h, w):
    rows, feats = text.shape[1:]
    n, chunk, cols = w[0].shape if step == 0 else w.shape[1:]
    vmem = pl.BlockSpec(memory_space=pltpu.VMEM)
    scratch = []
    if step == 0:
        scratch = [
            pltpu.VMEM((4, n, chunk, cols), jnp.bfloat16),
            pltpu.SemaphoreType.DMA((2, 4)),
        ]
        args, specs = [text, gain] + list(w), [vmem] * 2 + [pl.BlockSpec(memory_space=pl.ANY)] * 4
    else:
        args, specs = [text, gain, h, w], [vmem] * 4
    return pl.pallas_call(
        functools.partial(query_kernel, step),
        in_specs=[pl.BlockSpec(memory_space=pltpu.SMEM)] + specs,
        out_specs=[vmem] * 2,
        out_shape=[
            jax.ShapeDtypeStruct((n, cols // LANES * rows + EXTRA, LANES), jnp.bfloat16),
            jax.ShapeDtypeStruct((rows, feats), jnp.bfloat16),
        ],
        scratch_shapes=scratch,
        compiler_params=pltpu.CompilerParams(vmem_limit_bytes=VMEM_BYTES),
    )(ints, *args)


def keep(step, ints, kept_ref, new, old_ref):
    for o in range(kept_ref.shape[0]):
        old = jnp.zeros(new.shape, new.dtype) if old_ref is None else old_ref[o]
        kept_ref[o] = jnp.where(step - ints[0] == o, new, old)


def output_kernel(step, ints, p_ref, vo_ref, h_ref, *refs):
    o_ref, kept_ref = refs[-2:]
    probs = jnp.concatenate([p_ref[i] for i in range(p_ref.shape[0])], axis=1)
    new = h_ref[...].astype(jnp.float32) + dot16(probs, vo_ref[slot_of(step, ints, vo_ref.shape[0])])
    new = new.astype(jnp.bfloat16)
    o_ref[...] = new
    keep(step, ints, kept_ref, new, refs[0] if len(refs) == 3 else None)


def output(step, ints, probs, vo, h, kept):
    args = [probs, vo, h] + ([] if kept is None else [kept])
    return pl.pallas_call(
        functools.partial(output_kernel, step),
        in_specs=[pl.BlockSpec(memory_space=pltpu.SMEM)]
        + [pl.BlockSpec(memory_space=pltpu.VMEM)] * len(args),
        out_specs=[pl.BlockSpec(memory_space=pltpu.VMEM)] * 2,
        out_shape=[
            jax.ShapeDtypeStruct(h.shape, jnp.bfloat16),
            jax.ShapeDtypeStruct(vo.shape[:1] + h.shape, jnp.bfloat16),
        ],
        compiler_params=pltpu.CompilerParams(vmem_limit_bytes=VMEM_BYTES),
    )(ints, *args)


def own_lanes(rows):
    row = lax.broadcasted_iota(jnp.int32, (rows, LANES), 0)
    lane = lax.broadcasted_iota(jnp.int32, (rows, LANES), 1)
    return (lane == row) | (lane == row + rows), lane


def whole(shape):
    return pl.BlockSpec(shape, lambda *_: (0,) * len(shape))


def attend_kernel(step, width, ints, alpha_ref, gain_ref, k_ref, q_ref, *refs):
    p_ref, kept_ref = refs[-2:]
    slot = slot_of(step, ints, k_ref.shape[0])
    total = q_ref[0].astype(jnp.float32)
    for i in range(1, q_ref.shape[0]):
        total += q_ref[i].astype(jnp.float32)
    hd = gain_ref.shape[1]
    rows, cols = kept_ref.shape[1:]
    own, _ = own_lanes(rows)
    sums = jnp.broadcast_to(total[cols // hd * rows : cols // hd * rows + 1], (rows, LANES))
    ss = jnp.sum(jnp.where(own, sums, 0.0), axis=1, keepdims=True)
    rs = lax.rsqrt(ss / width + EPS)
    keys = k_ref[slot]
    row = lax.broadcasted_iota(jnp.int32, (rows, keys.shape[0]), 0)
    scale = jnp.where(row < ints[1 + slot], alpha_ref[0], 0.0)
    parts, normed = [], []
    for h in range(cols // hd):
        q = total[h * rows : (h + 1) * rows] * rs
        r = lax.rsqrt(jnp.mean(q * q, axis=1, keepdims=True) + EPS)
        qn = q * r * gain_ref[...] * (1.0 / math.sqrt(hd))
        normed.append(qn)
        sc = dot32(qn, keys, ROWS_ROWS)
        e = jnp.exp(sc - jnp.max(sc, axis=1, keepdims=True))
        parts.append(scale * e / jnp.sum(e, axis=1, keepdims=True))
    p = jnp.concatenate(parts, axis=1).astype(jnp.bfloat16)
    for i in range(p_ref.shape[0]):
        p_ref[i] = p
    old_ref = refs[0] if len(refs) == 3 else None
    keep(step, ints, kept_ref, jnp.concatenate(normed, axis=1), old_ref)


def attend(step, ints, alpha, width, gain, keys, parts, kept):
    hd = gain.shape[1]
    toks = keys.shape[1]
    heads = 4
    n = parts.shape[0]
    rows = (parts.shape[1] - EXTRA) // heads
    args = [gain, keys, parts] + ([] if kept is None else [kept])
    return pl.pallas_call(
        functools.partial(attend_kernel, step, width),
        in_specs=[pl.BlockSpec(memory_space=pltpu.SMEM)] * 2
        + [pl.BlockSpec(memory_space=pltpu.VMEM)] * len(args),
        out_specs=[pl.BlockSpec(memory_space=pltpu.VMEM)] * 2,
        out_shape=[
            jax.ShapeDtypeStruct((n, rows, heads * toks), jnp.bfloat16),
            jax.ShapeDtypeStruct(keys.shape[:1] + (rows, heads * hd), jnp.float32),
        ],
        compiler_params=pltpu.CompilerParams(vmem_limit_bytes=VMEM_BYTES),
    )(ints, alpha, *args)


def value_out_kernel(slots, v_ref, *refs):
    w_refs, o_ref = refs[:-1], refs[-1]
    n, vrows, hd = v_ref.shape
    toks = vrows // slots
    part, chunk = w_refs[0].shape[1] // hd, w_refs[0].shape[2]
    heads = part * len(w_refs) // 4

    def block(k, carry):
        v = v_ref[k]
        for h in range(heads):
            at = pl.multiple_of((k * heads + h) * toks, toks)
            for j in range(4):
                w_ref = w_refs[h // part * 4 + j]
                i = h % part * hd
                r = dot16(v, w_ref[k, i : i + hd, :]).astype(jnp.bfloat16)
                for o in range(slots):
                    o_ref[o, pl.ds(at, toks), j * chunk : (j + 1) * chunk] = r[
                        o * toks : (o + 1) * toks
                    ]
        return carry

    lax.fori_loop(0, n, block, 0)


def value_out(v, w, slots):
    n, vrows, hd = v.shape
    heads = w[0].shape[1] * len(w) // 4 // hd
    chunk = w[0].shape[2]
    toks = vrows // slots
    return pl.pallas_call(
        functools.partial(value_out_kernel, slots),
        in_specs=[pl.BlockSpec(memory_space=pltpu.VMEM)] * (1 + len(w)),
        out_specs=pl.BlockSpec(memory_space=pltpu.VMEM),
        out_shape=jax.ShapeDtypeStruct((slots, n * heads * toks, 4 * chunk), jnp.bfloat16),
        compiler_params=pltpu.CompilerParams(vmem_limit_bytes=VMEM_BYTES),
    )(v, *w)


def back_kernel(slot, qn_ref, k_ref, v_ref, raw_ref, da_ref, gain_ref, w_ref, o_ref):
    keys, vals, raw, gain = k_ref[slot], v_ref[slot], raw_ref[slot], gain_ref[...]
    hd = keys.shape[1]
    d_kn = jnp.zeros(keys.shape, jnp.float32)
    d_v = jnp.zeros(keys.shape, jnp.float32)
    for h in range(qn_ref.shape[2] // hd):
        qn = qn_ref[slot, :, h * hd : (h + 1) * hd]
        da = da_ref[slot, :, h * hd : (h + 1) * hd]
        sc = dot32(qn, keys, ROWS_ROWS)
        e = jnp.exp(sc - jnp.max(sc, axis=1, keepdims=True))
        p = e / jnp.sum(e, axis=1, keepdims=True)
        dp = dot32(da, vals, ROWS_ROWS)
        ds = p * (dp - jnp.sum(p * dp, axis=1, keepdims=True))
        d_kn += dot32(ds, qn, COLS_COLS)
        d_v += dot32(p, da, COLS_COLS)
    r = lax.rsqrt(jnp.mean(raw * raw, axis=1, keepdims=True) + EPS)
    u = d_kn * gain
    d_k = r * u - raw * (r * r * r * jnp.mean(raw * u, axis=1, keepdims=True))
    d_kv = jnp.concatenate([d_k, d_v], axis=1).astype(jnp.bfloat16)
    feats = o_ref.shape[2]
    for i in range(o_ref.shape[0]):
        part = dot16(d_kv, w_ref[i * feats : (i + 1) * feats], ROWS_ROWS)
        o_ref[i] = part.astype(jnp.bfloat16)


def back(slot, n, qn, keys, vals, raw, da, gain, w):
    args = (qn, keys, vals, raw, da, gain, w)
    return pl.pallas_call(
        functools.partial(back_kernel, slot),
        in_specs=[pl.BlockSpec(memory_space=pltpu.VMEM)] * len(args),
        out_specs=pl.BlockSpec(memory_space=pltpu.VMEM),
        out_shape=jax.ShapeDtypeStruct((n, keys.shape[1], w.shape[0] // n), jnp.bfloat16),
        compiler_params=pltpu.CompilerParams(vmem_limit_bytes=VMEM_BYTES),
    )(*args)


def pick(a, i, axis=0):
    return lax.dynamic_index_in_dim(a, i, axis, keepdims=False)


def after(x, *others):
    return lax.optimization_barrier((x,) + others)[0]


def swap(x, axis):
    return lax.all_to_all(x, axis, 0, 0, tiled=True)


def share(x, axis):
    return swap(jnp.broadcast_to(x[None], (lax.axis_size(axis),) + x.shape), axis)


def per_device(
    text, order, lengths, image, in_gain, wq, wk, wv, wo, query_norm_gain, k_gain, gate, cot
):
    D, S, T = lax.axis_size("dp"), lax.axis_size("section"), lax.axis_size("tensor")
    R = T // D
    d, s, t = lax.axis_index("dp"), lax.axis_index("section"), lax.axis_index("tensor")
    slots, rows = text.shape[:2]
    width = in_gain.shape[1]
    hd = k_gain.shape[1]
    feats = width // T
    chunk = feats // D
    toks = image.shape[1] * S

    def onward(x):
        return lax.ppermute(x, "section", [(i, (i + 1) % S) for i in range(S)])

    def dp_flip(x, m):
        return lax.ppermute(x, "dp", [(i, i ^ m) for i in range(D)])

    def dp_all(x):
        across = dp_flip(x, 2)
        return [x, dp_flip(x, 1), across, dp_flip(across, 1)]

    def spread(x):
        a, c = t // R, t % D
        parts = jnp.stack(jnp.split(x, D, axis=-1))
        got = []
        for k in range(D):
            pairs = [(i * R + b, b * D + (i + k) % D) for i in range(D) for b in range(R)]
            got.append(lax.ppermute(pick(parts, (a + k) % D), "tensor", pairs))
        got = jnp.stack(got)
        return jnp.concatenate([pick(got, (c - (d ^ j)) % D) for j in range(D)], axis=-1)

    def unspread(x):
        a, c = t // R, t % D
        parts = jnp.stack(jnp.split(x, D, axis=-1))
        got = []
        for k in range(D):
            pairs = [(b * D + (i + k) % D, i * R + b) for i in range(D) for b in range(R)]
            got.append(lax.ppermute(pick(parts, ((c - k) % D) ^ d), "tensor", pairs))
        got = jnp.stack(got)
        return jnp.concatenate([pick(got, (j - a) % D) for j in range(D)], axis=-1)

    micro = order[0]
    lens = jnp.take(lengths[0], micro)
    alpha = jnp.tanh(gate)

    wkv = jnp.concatenate([wk[0], wv[0]], axis=1)
    shared = share(after(jnp.take(image, micro, axis=0), wkv).reshape(-1, feats), "section")
    wkv = lax.all_gather(wkv, "dp", axis=0, tiled=True)

    wq_own = swap(after(wq[0].reshape(T, chunk, wq.shape[2]), shared), "tensor")
    wq_f = dp_all(wq_own)
    text_f = spread(after(jnp.take(text, micro, axis=0), shared))
    img = after(shared, wq_own).reshape(slots * toks, feats)
    img = lax.all_gather(img, "tensor", axis=1, tiled=True)
    gain_f = pick(in_gain.reshape(D, T, chunk), t, 1)
    gain_f = jnp.concatenate([pick(gain_f, d ^ j) for j in range(D)])[None]
    wo_own = jnp.moveaxis(wo[0].reshape(wo.shape[1], T, chunk), 1, 0)
    wo_own = after(wo_own, wq_own, wkv, text_f)
    half = wo_own.shape[1] // 2
    wo_a = swap(wo_own[:, :half], "tensor")
    wo_b = swap(after(wo_own[:, half:], wo_a, img), "tensor")
    kv = jnp.dot(img, wkv, preferred_element_type=jnp.float32)
    kv = jnp.moveaxis(kv.reshape(S, slots, toks // S, 2 * hd), 0, 1).reshape(slots, toks, 2 * hd)
    k_raw, vals = kv[..., :hd], kv[..., hd:]
    keys = k_raw * lax.rsqrt(jnp.mean(k_raw * k_raw, axis=-1, keepdims=True) + EPS) * k_gain[0]
    ints = jnp.concatenate([s.astype(jnp.int32)[None], lens])

    h = kept_qn = kept_h = None
    grads = []

    def image_part(slot):
        part = back(slot, T, kept_qn, keys, vals, k_raw, d_attn, k_gain, wkv)
        return jnp.sum(swap(part, "tensor").astype(jnp.float32), axis=0).astype(jnp.bfloat16)

    for step in range(S + slots - 1):
        parts, hq = query(step, ints, text_f, gain_f, h, wq_f if step == 0 else w)
        if step == 0:
            across = [dp_flip(own, 2) for own in (wo_a, wo_b)]
            parts = after(parts, across[0])
        swapped = swap(parts, "tensor")
        p, kept_qn = attend(step, ints, alpha, width, query_norm_gain, keys, swapped, kept_qn)
        if step == 0:
            vals16 = vals.astype(jnp.bfloat16).reshape(slots * toks, hd)
            vals16 = jnp.broadcast_to(vals16[None], (T,) + vals16.shape)
            both = swap(jnp.concatenate([after(p, across[1]), vals16], axis=1), "tensor")
            probs = both[:, :rows]
            wo_f = []
            for own, far in zip((wo_a, wo_b), across):
                wo_f += [own, dp_flip(own, 1), far, dp_flip(far, 1)]
            vo = value_out(both[:, rows:], wo_f, slots)
        else:
            probs = swap(after(p, *grads), "tensor")
        if step == 1:
            wo_full = lax.all_gather(after(wo[0], p), "dp", axis=1, tiled=True)
        if step == 5:
            mask = (jnp.arange(rows)[None, :] < lens[:, None]).astype(jnp.float32)[:, :, None]
            d_attn = dot16(cot[0].reshape(slots * rows, width), wo_full, ROWS_ROWS)
            d_attn = alpha[0] * mask * d_attn.reshape(slots, rows, -1)
            probs, d_attn = lax.optimization_barrier((probs, d_attn))
        if step >= S - 1:
            grads.append(image_part(step - S + 1))
        h, kept_h = output(step, ints, probs, vo, hq, kept_h)
        if step < S + slots - 2:
            w = fetch(ints, [after(own, h) for own in wq_f])
        h = onward(h)

    states = unspread(kept_h)
    grad = jnp.stack(grads).reshape(slots, S, toks // S, feats)
    grad = swap(jnp.moveaxis(grad, 1, 0), "section")
    grad = jnp.sum(grad.astype(jnp.float32), axis=0)
    grad = jnp.stack([pick(grad, jnp.argmax(micro == m)) for m in range(slots)])
    return (states[None], grad)


def solution(mesh):
    return jax.shard_map(
        per_device,
        mesh=mesh,
        in_specs=(
            P("dp", None, "tensor"),
            P("dp", None),
            P("dp", None),
            P("dp", "section", "tensor"),
            P("section", None),
            P("section", "dp", "tensor"),
            P("section", "dp", "tensor"),
            P("section", "dp", "tensor"),
            P("section", "tensor", "dp"),
            P("section", None),
            P("section", None),
            P("section"),
            P("section", "dp", None, None),
        ),
        out_specs=(P("section", "dp", None, "tensor"), P("dp", "section", "tensor")),
        check_vma=False,
    )
```

```python
import functools
import math

import jax
import jax.numpy as jnp
from jax import lax
from jax.experimental import pallas as pl
from jax.experimental.pallas import tpu as pltpu
from jax.sharding import PartitionSpec as P

EPS = 1e-05
HIGH = lax.Precision.HIGHEST
LANES = 128
EXTRA = 16
VMEM_BYTES = 14 * 2**20
ROWS_ROWS = (((1,), (1,)), ((), ()))
COLS_COLS = (((0,), (0,)), ((), ()))


def dot32(a, b, dims=(((1,), (0,)), ((), ()))):
    return lax.dot_general(a, b, dims, precision=HIGH, preferred_element_type=jnp.float32)


def dot16(a, b, dims=(((1,), (0,)), ((), ()))):
    return lax.dot_general(a, b, dims, preferred_element_type=jnp.float32)


def slot_of(step, ints, slots):
    return jnp.clip(step - ints[0], 0, slots - 1)


def fetch_kernel(*refs):
    ints, srcs, dst, sems = refs[0], refs[1:-2], refs[-2], refs[-1]
    copies = []
    for i in range(len(srcs)):
        size = srcs[i].shape[0] // 2
        for half in range(2):
            at = pl.ds(half * size, size)
            copies.append(pltpu.make_async_copy(srcs[i].at[at], dst.at[i, at], sems.at[i, half]))
            copies[-1].start()
    for copy in copies:
        copy.wait()


def fetch(ints, arrays):
    return pl.pallas_call(
        fetch_kernel,
        in_specs=[pl.BlockSpec(memory_space=pltpu.SMEM)]
        + [pl.BlockSpec(memory_space=pl.ANY)] * len(arrays),
        out_specs=pl.BlockSpec(memory_space=pltpu.VMEM),
        out_shape=pltpu.VMEM((len(arrays),) + arrays[0].shape, arrays[0].dtype),
        scratch_shapes=[pltpu.SemaphoreType.DMA((len(arrays), 2))],
        compiler_params=pltpu.CompilerParams(vmem_limit_bytes=VMEM_BYTES),
    )(ints, *arrays)


def query_kernel(step, ints, text_ref, gain_ref, *refs):
    copies = []
    if step == 0:
        w_refs, (q_ref, hq_ref, w_s, sems) = refs[:4], refs[4:]
        n = w_s.shape[1]
        for half in range(2):
            at = pl.ds(half * (n // 2), n // 2)
            for j in range(4):
                copy = pltpu.make_async_copy(w_refs[j].at[at], w_s.at[j, at], sems.at[half, j])
                copy.start()
                copies.append(copy)
    else:
        h_ref, w_s, q_ref, hq_ref = refs
    _, n, chunk, cols = w_s.shape
    h = text_ref[slot_of(step, ints, text_ref.shape[0])]
    if step > 0:
        h = jnp.where(ints[0] == 0, h, h_ref[...])
    hq_ref[...] = h
    hf = h.astype(jnp.float32)
    x = (hf * gain_ref[...]).astype(jnp.bfloat16)
    ss = jnp.sum(hf * hf, axis=1, keepdims=True)
    hi = ss.astype(jnp.bfloat16).astype(jnp.float32)
    rows = h.shape[0]
    own, lane = own_lanes(rows)
    pair = jnp.where(own, jnp.where(lane < rows, hi, ss - hi), 0.0)
    pair = jnp.broadcast_to(jnp.sum(pair, axis=0, keepdims=True), (EXTRA, LANES))
    pair = pair.astype(jnp.bfloat16)
    for k in range(n):
        if k % (n // 2) == 0:
            for copy in copies[k // (n // 2) * 4 :][:4]:
                copy.wait()
        acc = dot16(x[:, :chunk], w_s[0, k])
        for j in range(1, 4):
            acc += dot16(x[:, j * chunk : (j + 1) * chunk], w_s[j, k])
        acc = acc.astype(jnp.bfloat16)
        for i in range(cols // LANES):
            q_ref[k, i * rows : (i + 1) * rows, :] = acc[:, i * LANES : (i + 1) * LANES]
        q_ref[k, cols // LANES * rows :, :] = pair


def query(step, ints, text, gain, h, w):
    rows, feats = text.shape[1:]
    n, chunk, cols = w[0].shape if step == 0 else w.shape[1:]
    vmem = pl.BlockSpec(memory_space=pltpu.VMEM)
    scratch = []
    if step == 0:
        scratch = [
            pltpu.VMEM((4, n, chunk, cols), jnp.bfloat16),
            pltpu.SemaphoreType.DMA((2, 4)),
        ]
        args, specs = [text, gain] + list(w), [vmem] * 2 + [pl.BlockSpec(memory_space=pl.ANY)] * 4
    else:
        args, specs = [text, gain, h, w], [vmem] * 4
    return pl.pallas_call(
        functools.partial(query_kernel, step),
        in_specs=[pl.BlockSpec(memory_space=pltpu.SMEM)] + specs,
        out_specs=[vmem] * 2,
        out_shape=[
            jax.ShapeDtypeStruct((n, cols // LANES * rows + EXTRA, LANES), jnp.bfloat16),
            jax.ShapeDtypeStruct((rows, feats), jnp.bfloat16),
        ],
        scratch_shapes=scratch,
        compiler_params=pltpu.CompilerParams(vmem_limit_bytes=VMEM_BYTES),
    )(ints, *args)


def keep(step, ints, kept_ref, new, old_ref):
    for o in range(kept_ref.shape[0]):
        old = jnp.zeros(new.shape, new.dtype) if old_ref is None else old_ref[o]
        kept_ref[o] = jnp.where(step - ints[0] == o, new, old)


def output_kernel(step, ints, p_ref, vo_ref, h_ref, *refs):
    o_ref, kept_ref = refs[-2:]
    probs = jnp.concatenate([p_ref[i] for i in range(p_ref.shape[0])], axis=1)
    new = h_ref[...].astype(jnp.float32) + dot16(probs, vo_ref[slot_of(step, ints, vo_ref.shape[0])])
    new = new.astype(jnp.bfloat16)
    o_ref[...] = new
    keep(step, ints, kept_ref, new, refs[0] if len(refs) == 3 else None)


def output(step, ints, probs, vo, h, kept):
    args = [probs, vo, h] + ([] if kept is None else [kept])
    return pl.pallas_call(
        functools.partial(output_kernel, step),
        in_specs=[pl.BlockSpec(memory_space=pltpu.SMEM)]
        + [pl.BlockSpec(memory_space=pltpu.VMEM)] * len(args),
        out_specs=[pl.BlockSpec(memory_space=pltpu.VMEM)] * 2,
        out_shape=[
            jax.ShapeDtypeStruct(h.shape, jnp.bfloat16),
            jax.ShapeDtypeStruct(vo.shape[:1] + h.shape, jnp.bfloat16),
        ],
        compiler_params=pltpu.CompilerParams(vmem_limit_bytes=VMEM_BYTES),
    )(ints, *args)


def own_lanes(rows):
    row = lax.broadcasted_iota(jnp.int32, (rows, LANES), 0)
    lane = lax.broadcasted_iota(jnp.int32, (rows, LANES), 1)
    return (lane == row) | (lane == row + rows), lane


def whole(shape):
    return pl.BlockSpec(shape, lambda *_: (0,) * len(shape))


def attend_kernel(step, width, ints, alpha_ref, gain_ref, k_ref, q_ref, *refs):
    p_ref, kept_ref = refs[-2:]
    slot = slot_of(step, ints, k_ref.shape[0])
    total = q_ref[0].astype(jnp.float32)
    for i in range(1, q_ref.shape[0]):
        total += q_ref[i].astype(jnp.float32)
    hd = gain_ref.shape[1]
    rows, cols = kept_ref.shape[1:]
    own, _ = own_lanes(rows)
    sums = jnp.broadcast_to(total[cols // hd * rows : cols // hd * rows + 1], (rows, LANES))
    ss = jnp.sum(jnp.where(own, sums, 0.0), axis=1, keepdims=True)
    rs = lax.rsqrt(ss / width + EPS)
    keys = k_ref[slot]
    row = lax.broadcasted_iota(jnp.int32, (rows, keys.shape[0]), 0)
    scale = jnp.where(row < ints[1 + slot], alpha_ref[0], 0.0)
    parts, normed = [], []
    for h in range(cols // hd):
        q = total[h * rows : (h + 1) * rows] * rs
        r = lax.rsqrt(jnp.mean(q * q, axis=1, keepdims=True) + EPS)
        qn = q * r * gain_ref[...] * (1.0 / math.sqrt(hd))
        normed.append(qn)
        sc = dot32(qn, keys, ROWS_ROWS)
        e = jnp.exp(sc - jnp.max(sc, axis=1, keepdims=True))
        parts.append(scale * e / jnp.sum(e, axis=1, keepdims=True))
    p = jnp.concatenate(parts, axis=1).astype(jnp.bfloat16)
    for i in range(p_ref.shape[0]):
        p_ref[i] = p
    old_ref = refs[0] if len(refs) == 3 else None
    keep(step, ints, kept_ref, jnp.concatenate(normed, axis=1), old_ref)


def attend(step, ints, alpha, width, gain, keys, parts, kept):
    hd = gain.shape[1]
    toks = keys.shape[1]
    heads = 4
    n = parts.shape[0]
    rows = (parts.shape[1] - EXTRA) // heads
    args = [gain, keys, parts] + ([] if kept is None else [kept])
    return pl.pallas_call(
        functools.partial(attend_kernel, step, width),
        in_specs=[pl.BlockSpec(memory_space=pltpu.SMEM)] * 2
        + [pl.BlockSpec(memory_space=pltpu.VMEM)] * len(args),
        out_specs=[pl.BlockSpec(memory_space=pltpu.VMEM)] * 2,
        out_shape=[
            jax.ShapeDtypeStruct((n, rows, heads * toks), jnp.bfloat16),
            jax.ShapeDtypeStruct(keys.shape[:1] + (rows, heads * hd), jnp.float32),
        ],
        compiler_params=pltpu.CompilerParams(vmem_limit_bytes=VMEM_BYTES),
    )(ints, alpha, *args)


def value_out_kernel(slots, v_ref, *refs):
    w_refs, o_ref = refs[:-1], refs[-1]
    n, vrows, hd = v_ref.shape
    toks = vrows // slots
    part, chunk = w_refs[0].shape[1] // hd, w_refs[0].shape[2]
    heads = part * len(w_refs) // 4

    def block(k, carry):
        v = v_ref[k]
        for h in range(heads):
            at = pl.multiple_of((k * heads + h) * toks, toks)
            for j in range(4):
                w_ref = w_refs[h // part * 4 + j]
                i = h % part * hd
                r = dot16(v, w_ref[k, i : i + hd, :]).astype(jnp.bfloat16)
                for o in range(slots):
                    o_ref[o, pl.ds(at, toks), j * chunk : (j + 1) * chunk] = r[
                        o * toks : (o + 1) * toks
                    ]
        return carry

    lax.fori_loop(0, n, block, 0)


def value_out(v, w, slots):
    n, vrows, hd = v.shape
    heads = w[0].shape[1] * len(w) // 4 // hd
    chunk = w[0].shape[2]
    toks = vrows // slots
    return pl.pallas_call(
        functools.partial(value_out_kernel, slots),
        in_specs=[pl.BlockSpec(memory_space=pltpu.VMEM)] * (1 + len(w)),
        out_specs=pl.BlockSpec(memory_space=pltpu.VMEM),
        out_shape=jax.ShapeDtypeStruct((slots, n * heads * toks, 4 * chunk), jnp.bfloat16),
        compiler_params=pltpu.CompilerParams(vmem_limit_bytes=VMEM_BYTES),
    )(v, *w)


def back_kernel(slot, qn_ref, k_ref, v_ref, raw_ref, da_ref, gain_ref, w_ref, o_ref):
    keys, vals, raw, gain = k_ref[slot], v_ref[slot], raw_ref[slot], gain_ref[...]
    hd = keys.shape[1]
    d_kn = jnp.zeros(keys.shape, jnp.float32)
    d_v = jnp.zeros(keys.shape, jnp.float32)
    for h in range(qn_ref.shape[2] // hd):
        qn = qn_ref[slot, :, h * hd : (h + 1) * hd]
        da = da_ref[slot, :, h * hd : (h + 1) * hd]
        sc = dot32(qn, keys, ROWS_ROWS)
        e = jnp.exp(sc - jnp.max(sc, axis=1, keepdims=True))
        p = e / jnp.sum(e, axis=1, keepdims=True)
        dp = dot32(da, vals, ROWS_ROWS)
        ds = p * (dp - jnp.sum(p * dp, axis=1, keepdims=True))
        d_kn += dot32(ds, qn, COLS_COLS)
        d_v += dot32(p, da, COLS_COLS)
    r = lax.rsqrt(jnp.mean(raw * raw, axis=1, keepdims=True) + EPS)
    u = d_kn * gain
    d_k = r * u - raw * (r * r * r * jnp.mean(raw * u, axis=1, keepdims=True))
    d_kv = jnp.concatenate([d_k, d_v], axis=1).astype(jnp.bfloat16)
    feats = o_ref.shape[2]
    for i in range(o_ref.shape[0]):
        part = dot16(d_kv, w_ref[i * feats : (i + 1) * feats], ROWS_ROWS)
        o_ref[i] = part.astype(jnp.bfloat16)


def back(slot, n, qn, keys, vals, raw, da, gain, w):
    args = (qn, keys, vals, raw, da, gain, w)
    return pl.pallas_call(
        functools.partial(back_kernel, slot),
        in_specs=[pl.BlockSpec(memory_space=pltpu.VMEM)] * len(args),
        out_specs=pl.BlockSpec(memory_space=pltpu.VMEM),
        out_shape=jax.ShapeDtypeStruct((n, keys.shape[1], w.shape[0] // n), jnp.bfloat16),
        compiler_params=pltpu.CompilerParams(vmem_limit_bytes=VMEM_BYTES),
    )(*args)


def pick(a, i, axis=0):
    return lax.dynamic_index_in_dim(a, i, axis, keepdims=False)


def after(x, *others):
    return lax.optimization_barrier((x,) + others)[0]


def swap(x, axis):
    return lax.all_to_all(x, axis, 0, 0, tiled=True)


def share(x, axis):
    return swap(jnp.broadcast_to(x[None], (lax.axis_size(axis),) + x.shape), axis)


def per_device(
    text, order, lengths, image, in_gain, wq, wk, wv, wo, query_norm_gain, k_gain, gate, cot
):
    D, S, T = lax.axis_size("dp"), lax.axis_size("section"), lax.axis_size("tensor")
    R = T // D
    d, s, t = lax.axis_index("dp"), lax.axis_index("section"), lax.axis_index("tensor")
    slots, rows = text.shape[:2]
    width = in_gain.shape[1]
    hd = k_gain.shape[1]
    feats = width // T
    chunk = feats // D
    toks = image.shape[1] * S

    def onward(x):
        return lax.ppermute(x, "section", [(i, (i + 1) % S) for i in range(S)])

    def dp_flip(x, m):
        return lax.ppermute(x, "dp", [(i, i ^ m) for i in range(D)])

    def dp_all(x):
        across = dp_flip(x, 2)
        return [x, dp_flip(x, 1), across, dp_flip(across, 1)]

    def spread(x):
        a, c = t // R, t % D
        parts = jnp.stack(jnp.split(x, D, axis=-1))
        got = []
        for k in range(D):
            pairs = [(i * R + b, b * D + (i + k) % D) for i in range(D) for b in range(R)]
            got.append(lax.ppermute(pick(parts, (a + k) % D), "tensor", pairs))
        got = jnp.stack(got)
        return jnp.concatenate([pick(got, (c - (d ^ j)) % D) for j in range(D)], axis=-1)

    def unspread(x):
        a, c = t // R, t % D
        parts = jnp.stack(jnp.split(x, D, axis=-1))
        got = []
        for k in range(D):
            pairs = [(b * D + (i + k) % D, i * R + b) for i in range(D) for b in range(R)]
            got.append(lax.ppermute(pick(parts, ((c - k) % D) ^ d), "tensor", pairs))
        got = jnp.stack(got)
        return jnp.concatenate([pick(got, (j - a) % D) for j in range(D)], axis=-1)

    micro = order[0]
    lens = jnp.take(lengths[0], micro)
    alpha = jnp.tanh(gate)

    wkv = jnp.concatenate([wk[0], wv[0]], axis=1)
    shared = share(after(jnp.take(image, micro, axis=0), wkv).reshape(-1, feats), "section")
    wkv = lax.all_gather(wkv, "dp", axis=0, tiled=True)

    wq_own = swap(after(wq[0].reshape(T, chunk, wq.shape[2]), shared), "tensor")
    wq_f = dp_all(wq_own)
    text_f = spread(after(jnp.take(text, micro, axis=0), shared))
    img = after(shared, wq_own).reshape(slots * toks, feats)
    img = lax.all_gather(img, "tensor", axis=1, tiled=True)
    gain_f = pick(in_gain.reshape(D, T, chunk), t, 1)
    gain_f = jnp.concatenate([pick(gain_f, d ^ j) for j in range(D)])[None]
    wo_own = jnp.moveaxis(wo[0].reshape(wo.shape[1], T, chunk), 1, 0)
    wo_own = after(wo_own, wq_own, wkv, text_f)
    half = wo_own.shape[1] // 2
    wo_a = swap(wo_own[:, :half], "tensor")
    wo_b = swap(after(wo_own[:, half:], wo_a, img), "tensor")
    kv = jnp.dot(img, wkv, preferred_element_type=jnp.float32)
    kv = jnp.moveaxis(kv.reshape(S, slots, toks // S, 2 * hd), 0, 1).reshape(slots, toks, 2 * hd)
    k_raw, vals = kv[..., :hd], kv[..., hd:]
    keys = k_raw * lax.rsqrt(jnp.mean(k_raw * k_raw, axis=-1, keepdims=True) + EPS) * k_gain[0]
    ints = jnp.concatenate([s.astype(jnp.int32)[None], lens])

    h = kept_qn = kept_h = None
    grads = []

    def image_part(slot):
        part = back(slot, T, kept_qn, keys, vals, k_raw, d_attn, k_gain, wkv)
        return jnp.sum(swap(part, "tensor").astype(jnp.float32), axis=0).astype(jnp.bfloat16)

    for step in range(S + slots - 1):
        parts, hq = query(step, ints, text_f, gain_f, h, wq_f if step == 0 else w)
        if step == 0:
            across = [dp_flip(own, 2) for own in (wo_a, after(wo_b, hq))]
            parts = after(parts, across[0])
        swapped = swap(parts, "tensor")
        p, kept_qn = attend(step, ints, alpha, width, query_norm_gain, keys, swapped, kept_qn)
        if step == 0:
            vals16 = vals.astype(jnp.bfloat16).reshape(slots * toks, hd)
            vals16 = jnp.broadcast_to(vals16[None], (T,) + vals16.shape)
            both = swap(jnp.concatenate([after(p, across[1]), vals16], axis=1), "tensor")
            probs = both[:, :rows]
            wo_f = []
            for own, far in zip((wo_a, wo_b), across):
                wo_f += [own, dp_flip(own, 1), far, dp_flip(far, 1)]
            vo = value_out(both[:, rows:], wo_f, slots)
        else:
            probs = swap(after(p, *grads), "tensor")
        if step == 1:
            wo_full = lax.all_gather(after(wo[0], p), "dp", axis=1, tiled=True)
        if step == 5:
            mask = (jnp.arange(rows)[None, :] < lens[:, None]).astype(jnp.float32)[:, :, None]
            d_attn = dot16(cot[0].reshape(slots * rows, width), wo_full, ROWS_ROWS)
            d_attn = alpha[0] * mask * d_attn.reshape(slots, rows, -1)
            probs, d_attn = lax.optimization_barrier((probs, d_attn))
        if step >= S - 1:
            grads.append(image_part(step - S + 1))
        h, kept_h = output(step, ints, probs, vo, hq, kept_h)
        if step < S + slots - 2:
            w = fetch(ints, [after(own, h) for own in wq_f])
        h = onward(h)

    states = unspread(kept_h)
    grad = jnp.stack(grads).reshape(slots, S, toks // S, feats)
    grad = swap(jnp.moveaxis(grad, 1, 0), "section")
    grad = jnp.sum(grad.astype(jnp.float32), axis=0)
    grad = jnp.stack([pick(grad, jnp.argmax(micro == m)) for m in range(slots)])
    return (states[None], grad)


def solution(mesh):
    return jax.shard_map(
        per_device,
        mesh=mesh,
        in_specs=(
            P("dp", None, "tensor"),
            P("dp", None),
            P("dp", None),
            P("dp", "section", "tensor"),
            P("section", None),
            P("section", "dp", "tensor"),
            P("section", "dp", "tensor"),
            P("section", "dp", "tensor"),
            P("section", "tensor", "dp"),
            P("section", None),
            P("section", None),
            P("section"),
            P("section", "dp", None, None),
        ),
        out_specs=(P("section", "dp", None, "tensor"), P("dp", "section", "tensor")),
        check_vma=False,
    )
```
